128 devices in a mesh: dp: 32 (over x, y, core), cent: 4 (over z).
Axes of the slice: x: 4, y: 4, z: 4, core: 2. Of those that a mesh axis runs over, the one named last changes fastest.
Arguments:
- embeddings: bfloat16 [131072, 768], P(('dp', 'cent')), may hold values from -40 to 40
- init_centroids: bfloat16 [2048, 768], P('cent'), may hold values from -40 to 40
- assign: int32 [131072], P(('dp', 'cent')), may hold values from 0 to 2047, as said below
- owner_map: int32 [2048], replicated, may hold values from 0 to 127, as said below
Outputs:
- centroids: float32 [2048, 768], P('cent')
- similarity: bfloat16 [128, 2048, 2048], P(('dp', 'cent'))
The draws below stay inside these ranges and needn't reach their ends.
Inputs may be any that keep to these rules, and one draw needn't show every extreme that they name: `assign`: the rows of one device send at most 16 rows to one owner (owner_map of the row's cluster); in every draw some owner receives exactly 16 rows from every device. `owner_map`: every owner owns the same number of clusters.
All inputs are finite; a program needn't handle non-finite values.
Results may differ from the reference program's by a relative error of at most 0.018.
Values may be sent and summed in bfloat16 or wider, within the bound.
No kernel may reach another device: no remote copies, remote signals or barrier semaphores. Data moves between devices by JAX's collectives and lax.ppermute only.
A program may use at most 64 MiB of HBM per device.

```python
import math
import jax
import jax.numpy as jnp
from jax import lax

D = 768
K = 2048
ROUNDS = 2
ROW_DEV = 1024
ROWS = 131072
N_DP = 32
N_CENT = 4


def cluster_table(key):
    table_key = jax.random.fold_in(key, 101)
    sort_permutation = jax.random.permutation(table_key, K).astype(jnp.int32)
    busiest = jax.random.permutation(jax.random.fold_in(table_key, 1), N_DP * N_CENT)[:2].astype(jnp.int32)
    return (sort_permutation, busiest)


def draw_owner_map(key, part):
    sort_permutation, busiest = cluster_table(key)
    vectors_per_holder = K // (N_DP * N_CENT)
    owned = (jnp.arange(K, dtype=jnp.int32) // vectors_per_holder).astype(jnp.int32)
    return jnp.zeros((K,), jnp.int32).at[sort_permutation].set(owned)


def draw_assign(key, part):
    sort_permutation, busiest = cluster_table(key)
    key = jax.random.fold_in(key, 5)
    devices = N_DP * N_CENT
    capacity = 2 * ROW_DEV // devices
    vectors_per_holder = K // devices
    key_offset, key_shuffle, key_chosen = jax.random.split(key, 3)
    is_busy = jnp.zeros((devices,), jnp.int32).at[busiest].set(1)
    others = jnp.argsort(is_busy * devices + jnp.arange(devices, dtype=jnp.int32), stable=True)[:devices - 2].astype(jnp.int32)
    offsets = jax.random.randint(key_offset, (devices, 1), 0, devices - 2)
    position_within = jnp.arange(ROW_DEV, dtype=jnp.int32)[None, :]
    spread = others[(offsets + position_within - 2 * capacity) % (devices - 2)]
    targets = jnp.where(position_within < capacity, busiest[0], jnp.where(position_within < 2 * capacity, busiest[1], spread))
    shuffles = jax.vmap(lambda single: jax.random.permutation(single, ROW_DEV))(jax.random.split(key_shuffle, devices))
    targets = jnp.take_along_axis(targets, shuffles.astype(jnp.int32), axis=1)
    chosen = jax.random.randint(key_chosen, (devices, ROW_DEV), 0, vectors_per_holder)
    cluster = sort_permutation[targets * vectors_per_holder + chosen]
    return cluster.reshape(-1).astype(jnp.int32)


def draw_embeddings(key, part):
    key = jax.random.fold_in(key, 11)
    key_scale, key_pattern = jax.random.split(key, 2)
    row_scale = jnp.exp(jax.random.uniform(key_scale, (ROWS, 1), jnp.float32, 0.0, math.log(10.0)))
    pattern = jnp.clip(jax.random.normal(key_pattern, (ROWS, D), jnp.float32), -4.0, 4.0)
    return (pattern * row_scale).astype(jnp.bfloat16)


def draw_init_centroids(key, part):
    key = jax.random.fold_in(key, 13)
    key_scale, key_pattern = jax.random.split(key, 2)
    row_scale = jnp.exp(jax.random.uniform(key_scale, (K, 1), jnp.float32, 0.0, math.log(10.0)))
    pattern = jnp.clip(jax.random.normal(key_pattern, (K, D), jnp.float32), -4.0, 4.0)
    return (pattern * row_scale).astype(jnp.bfloat16)


def setup_inputs(seed: int = 0) -> dict:
    keys = jax.random.split(jax.random.key(seed), 5)
    return {
        "embeddings": draw_embeddings(jax.random.fold_in(keys[4], 71), 0),
        "init_centroids": draw_init_centroids(jax.random.fold_in(keys[4], 71), 0),
        "assign": draw_assign(jax.random.fold_in(keys[4], 71), 0),
        "owner_map": draw_owner_map(jax.random.fold_in(keys[4], 71), 0),
    }


epsilon = 1e-06
logit_divisor = 0.02

def normalize_rows(matrix):
    wide = matrix.astype(jnp.float32)
    return (wide / jnp.sqrt(lax.optimization_barrier(jnp.sum(wide * wide, axis=-1, keepdims=True)) + epsilon)).astype(jnp.bfloat16)

def product(left, right):
    return jnp.dot(left.astype(jnp.float32), right.astype(jnp.float32).T, precision=lax.Precision.HIGHEST)

def soft_round(unit_rows, present_centroids):
    devices = N_DP * N_CENT
    row_blocks = unit_rows.reshape(devices, ROW_DEV, D)

    def accumulate(running, row_block):
        cosine_tile = product(row_block, present_centroids)
        softmax_membership = jnp.exp(cosine_tile / logit_divisor)
        weights = (softmax_membership / lax.optimization_barrier(jnp.sum(softmax_membership, axis=1, keepdims=True))).astype(jnp.bfloat16)
        return (running + product(weights.T, row_block.T), None)
    initial = jnp.zeros((K, D), jnp.float32)
    totals, _ = lax.scan(accumulate, initial, row_blocks)
    return normalize_rows(totals)

def reference(embeddings, init_centroids, assign, owner_map):
    unit_rows = normalize_rows(embeddings)
    present_centroids = normalize_rows(init_centroids)
    for round_index in range(ROUNDS):
        present_centroids = soft_round(unit_rows, present_centroids)
    centroids = present_centroids.astype(jnp.float32) * math.sqrt(D)
    devices = N_DP * N_CENT
    capacity = 2 * ROW_DEV // devices
    owners = owner_map[assign].astype(jnp.int32)
    per_source = owners.reshape(devices, ROW_DEV)
    owner_hits = (per_source[:, :, None] == jnp.arange(devices, dtype=jnp.int32)[None, None, :]).astype(jnp.int32)
    slot_index = lax.optimization_barrier(jnp.sum(jnp.cumsum(owner_hits, axis=1) * owner_hits, axis=2)) - 1
    source = jnp.arange(devices, dtype=jnp.int32)[:, None]
    position = (per_source * (devices * capacity) + source * capacity + slot_index).reshape(-1).astype(jnp.int32)
    buffer = jnp.zeros((devices * 2 * ROW_DEV, D), jnp.bfloat16).at[position].set(unit_rows)
    labels = jnp.full((devices * 2 * ROW_DEV,), -1, jnp.int32).at[position].set(assign)
    main_diagonal = jnp.eye(2 * ROW_DEV, dtype=bool)

    def similar(holder_couple):
        row_block, labels_of = holder_couple
        inner = product(row_block, row_block) * math.sqrt(D)
        same_cluster = (labels_of[:, None] == labels_of[None, :]) & (labels_of[:, None] >= 0) & jnp.logical_not(main_diagonal)
        return jnp.where(same_cluster, inner, 0.0).astype(jnp.bfloat16)
    similarity = lax.map(similar, (buffer.reshape(devices, 2 * ROW_DEV, D), labels.reshape(devices, 2 * ROW_DEV)))
    return (centroids, similarity)
```

```python
import math

import jax
import jax.numpy as jnp
from jax import lax
from jax.sharding import PartitionSpec as P

ROUNDS = 2
AXES = ("dp", "cent")

epsilon = 1e-06
logit_divisor = 0.02


def normalize_rows(matrix):
    wide = matrix.astype(jnp.float32)
    return (wide / jnp.sqrt(jnp.sum(wide * wide, axis=-1, keepdims=True) + epsilon)).astype(
        jnp.bfloat16
    )


def contract_final_axis(left, right):
    return lax.dot_general(
        left, right, (((1,), (1,)), ((), ())), preferred_element_type=jnp.float32
    )


def device_number(plane, core, depth, cent_count):
    return (plane * 2 + core) * cent_count + depth


def plan(dp_count, cent_count):
    planes = dp_count // 2
    spots = [
        (p, c, z) for p in range(planes) for c in range(2) for z in range(cent_count)
    ]

    def moved(core_step, depth_step):
        return [
            (
                device_number(p, c, z, cent_count),
                device_number(p, (c + core_step) % 2, (z + depth_step) % cent_count, cent_count),
            )
            for p, c, z in spots
        ]

    plane_groups = [
        [device_number(p, c, z, cent_count) for p in range(planes)]
        for c in range(2)
        for z in range(cent_count)
    ]
    return moved, plane_groups


def shards(embeddings, init_centroids, assign, owner_map):
    devices = lax.axis_size(AXES)
    cent_count = lax.axis_size("cent")
    dp_count = lax.axis_size("dp")
    planes = dp_count // 2
    moved, plane_groups = plan(dp_count, cent_count)
    core = lax.axis_index("dp") % 2

    def send(value, core_step, depth_step):
        return lax.ppermute(value, AXES, moved(core_step, depth_step))

    unit_rows = normalize_rows(embeddings)
    local_rows, feature_width = unit_rows.shape
    block_size = init_centroids.shape[0]
    half = block_size // 2
    share = half // planes
    centroid_half = normalize_rows(lax.dynamic_slice_in_dim(init_centroids, core * half, half, 0))

    cut = local_rows // 2
    first, second = unit_rows[:cut], unit_rows[cut:]
    below_first, above_second = send(first, 0, 1), send(second, 0, -1)
    below_second, above_first = send(second, 0, 1), send(first, 0, -1)
    far_first, far_second = send(below_first, 0, 1), send(above_second, 0, -1)
    pieces = [first, second, above_first, above_second, far_first, far_second, below_first, below_second]
    own = jnp.concatenate(pieces)
    other = jnp.concatenate([send(piece, 1, 0) for piece in pieces])
    rows = jnp.concatenate([own, other])
    group_rows = own.shape[0]

    def total_over_group(partial):
        mine, theirs = partial[:group_rows], partial[group_rows:]
        swapped = send(partial, 1, 0)
        chip = jnp.stack([mine + swapped[group_rows:], theirs + swapped[:group_rows]])
        result = chip
        for step in range(1, cent_count):
            result = result + jnp.roll(send(chip, 0, -step), step * local_rows, axis=1)
        return result.reshape(-1)

    for round_index in range(ROUNDS):
        scores = contract_final_axis(centroid_half, rows)
        membership = jnp.exp(scores / logit_divisor)
        total = total_over_group(jnp.sum(membership, axis=0))
        weights = (membership / total[None, :]).astype(jnp.bfloat16)
        partial = jnp.dot(weights, rows, preferred_element_type=jnp.float32).astype(jnp.bfloat16)
        arrived = lax.all_to_all(
            partial.reshape(planes, share, feature_width),
            AXES,
            0,
            0,
            axis_index_groups=plane_groups,
            tiled=True,
        )
        unit_share = normalize_rows(jnp.sum(arrived.astype(jnp.float32), axis=0))
        spread = lax.optimization_barrier(
            jnp.broadcast_to(unit_share[None], (planes, share, feature_width))
        )
        centroid_half = lax.all_to_all(
            spread, AXES, 0, 0, axis_index_groups=plane_groups, tiled=True
        ).reshape(half, feature_width)
    sibling_half = send(centroid_half, 1, 0)
    centroids = jnp.where(
        core == 0,
        jnp.concatenate([centroid_half, sibling_half]),
        jnp.concatenate([sibling_half, centroid_half]),
    ).astype(jnp.float32) * math.sqrt(feature_width)

    cluster_count = owner_map.shape[0]
    capacity = 2 * local_rows // devices
    matches = assign[:, None] == jnp.arange(cluster_count, dtype=jnp.int32)[None, :]
    owner_of = jnp.sum(jnp.where(matches, owner_map[None, :], 0), axis=1)
    owner_hits = owner_of[:, None] == jnp.arange(devices, dtype=jnp.int32)[None, :]
    earlier = (
        jnp.arange(local_rows)[:, None] > jnp.arange(local_rows)[None, :]
    ).astype(jnp.bfloat16)
    counts = jnp.dot(
        earlier, owner_hits.astype(jnp.bfloat16), preferred_element_type=jnp.float32
    )
    slot_index = jnp.sum(jnp.where(owner_hits, counts, 0.0), axis=1).astype(jnp.int32)
    position = owner_of * capacity + slot_index
    taken = position[None, :] == jnp.arange(devices * capacity, dtype=jnp.int32)[:, None]
    send_rows = jnp.dot(
        taken.astype(jnp.bfloat16), unit_rows, preferred_element_type=jnp.float32
    ).astype(jnp.bfloat16)
    send_labels = jnp.sum(jnp.where(taken, assign[None, :] + 1, 0), axis=1) - 1
    received = lax.all_to_all(
        send_rows.reshape(devices, capacity, feature_width), AXES, 0, 0, tiled=True
    ).reshape(-1, feature_width)
    labels_of = lax.all_to_all(
        send_labels.reshape(devices, capacity), AXES, 0, 0, tiled=True
    ).reshape(-1)
    inner = contract_final_axis(received, received) * math.sqrt(feature_width)
    main_diagonal = jnp.eye(received.shape[0], dtype=bool)
    same_cluster = (
        (labels_of[:, None] == labels_of[None, :])
        & (labels_of[:, None] >= 0)
        & jnp.logical_not(main_diagonal)
    )
    similarity = jnp.where(same_cluster, inner, 0.0).astype(jnp.bfloat16)[None]
    return (centroids, similarity)


def solution(mesh):
    return jax.shard_map(
        shards,
        mesh=mesh,
        in_specs=(P(AXES, None), P("cent", None), P(AXES), P()),
        out_specs=(P("cent", None), P(AXES, None, None)),
        check_vma=False,
    )
```

```python
import functools
import math

import jax
import jax.numpy as jnp
from jax import lax
from jax.experimental import pallas as pl
from jax.experimental.pallas import tpu as pltpu
from jax.sharding import PartitionSpec as P

ROUNDS = 2
AXES = ("dp", "cent")

epsilon = 1e-06
logit_divisor = 0.02
MIB = 1024 * 1024
LABEL_LANES = 128
NEAR_COST = 1_000_000
FAR_COST = 25_000_000_000
FULL = 61


def unit(matrix):
    wide = matrix.astype(jnp.float32)
    return wide / jnp.sqrt(jnp.sum(wide * wide, axis=-1, keepdims=True) + epsilon)


def normalize_rows(matrix):
    return unit(matrix).astype(jnp.bfloat16)


def contract_final_axis(left, right):
    return lax.dot_general(
        left, right, (((1,), (1,)), ((), ())), preferred_element_type=jnp.float32
    )


def whole():
    return pl.BlockSpec(memory_space=pltpu.VMEM)


def in_hbm():
    return pl.BlockSpec(memory_space=pl.ANY)


def call(kernel, name, vmem, flops, **options):
    return pl.pallas_call(
        kernel,
        name=name,
        cost_estimate=pl.CostEstimate(flops=int(flops), bytes_accessed=1 << 20, transcendentals=0),
        compiler_params=pltpu.CompilerParams(vmem_limit_bytes=vmem * MIB),
        **options,
    )


def membership_of(block, rows, scale):
    scores = contract_final_axis(block, rows)
    membership = jnp.exp2(scores * (scale * (math.log2(math.e) / logit_divisor)))
    return membership.astype(jnp.bfloat16), jnp.sum(membership, axis=0, keepdims=True)


def piece_kernel(raw_ref, block_ref, member_ref, total_ref, scale_ref):
    wide = raw_ref[...].astype(jnp.float32)
    squares = jnp.sum(wide * wide, axis=-1, keepdims=True) + epsilon
    scale = (1.0 / jnp.sqrt(jnp.broadcast_to(squares, (squares.shape[0], 8)))).T[:1]
    scale_ref[...] = scale
    member_ref[...], total_ref[...] = membership_of(block_ref[...], raw_ref[...], scale)


def score_piece(raw, block, cost):
    size, width = raw.shape
    count = block.shape[0]
    line = jax.ShapeDtypeStruct((1, size), jnp.float32)
    return call(
        piece_kernel,
        "score_piece",
        12,
        cost,
        in_specs=[whole(), whole()],
        out_specs=[whole()] * 3,
        out_shape=[jax.ShapeDtypeStruct((count, size), jnp.bfloat16), line, line],
    )(raw, block)


def fetches(sources, taken, sems):
    size = sources[1].shape[0]
    parts = [sources[0].at[pl.ds(0, size)], sources[0].at[pl.ds(size, size)]] + list(sources[1:])
    return [
        pltpu.make_async_copy(part, taken.at[pl.ds(i * size, size)], sems.at[i])
        for i, part in enumerate(parts)
    ]


def score_kernel(pieces, scale_ref, own_ref, other_ref, *rest):
    sources, outs = rest[: pieces - 1], rest[pieces - 1 :]
    member_refs, total_ref = outs[:pieces], outs[pieces]
    taken, members, block, in_sem, out_sem = outs[pieces + 1 :]
    half = own_ref.shape[0]
    size = sources[1].shape[0]
    arriving = fetches(sources, taken, in_sem)
    for copy in arriving:
        copy.start()
    block[:half], block[half:] = own_ref[...], other_ref[...]
    leaving = []
    for i in range(pieces):
        arriving[i].wait()
        at = slice(i * size, (i + 1) * size)
        members[i], total_ref[:, at] = membership_of(block[...], taken[at], scale_ref[:, at])
        leaving.append(pltpu.make_async_copy(members.at[i], member_refs[i], out_sem.at[i]))
        leaving[-1].start()
    for copy in leaving:
        copy.wait()


def score_rows(sources, scale, own_half, other_half):
    pieces = len(sources) + 1
    size, width = sources[1].shape
    count = 2 * own_half.shape[0]
    each = pltpu.SemaphoreType.DMA((pieces,))
    out = call(
        functools.partial(score_kernel, pieces),
        "score_rows",
        FULL,
        2 * pieces * size * width * count,
        in_specs=[whole()] * 3 + [in_hbm()] * len(sources),
        out_specs=[in_hbm()] * pieces + [whole()],
        out_shape=[jax.ShapeDtypeStruct((count, size), jnp.bfloat16)] * pieces
        + [jax.ShapeDtypeStruct((1, pieces * size), jnp.float32)],
        scratch_shapes=[
            pltpu.VMEM((pieces * size, width), jnp.bfloat16),
            pltpu.VMEM((pieces, count, size), jnp.bfloat16),
            pltpu.VMEM((count, width), jnp.bfloat16),
            each,
            each,
        ],
    )(scale, own_half, other_half, *sources)
    return out[:pieces], out[pieces]


def sum_kernel(pieces, depth, scale_ref, *rest):
    total_refs, rest = rest[:depth], rest[depth:]
    member_refs, sources = rest[:pieces], rest[pieces : 2 * pieces - 1]
    own_ref, other_ref, members, taken, running, member_sem, row_sem = rest[-7:]
    half = own_ref.shape[0]
    size = sources[1].shape[0]
    arriving = [
        (rows, pltpu.make_async_copy(member_refs[i], members.at[i], member_sem.at[i]))
        for i, rows in enumerate(fetches(sources, taken, row_sem))
    ]
    for pair in arriving:
        for copy in pair:
            copy.start()
    for i in range(pieces):
        for copy in arriving[i]:
            copy.wait()
        at = slice(i * size, (i + 1) * size)
        total = total_refs[0][:, at]
        for k in range(1, depth):
            j = (i + pieces - k * (pieces // depth)) % pieces
            total = total + total_refs[k][:, j * size : (j + 1) * size]
        weights = members[i].astype(jnp.float32) * (scale_ref[:, at] / total)
        product = jnp.dot(
            weights.astype(jnp.bfloat16), taken[at], preferred_element_type=jnp.float32
        )
        if i == 0:
            running[...] = product
        else:
            running[...] += product
    own_ref[...] = running[:half].astype(jnp.bfloat16)
    other_ref[...] = running[half:].astype(jnp.bfloat16)


def weighted_sums(members, sources, scale, totals, after):
    pieces = len(members)
    count, size = members[0].shape
    width = sources[0].shape[1]
    sums = jax.ShapeDtypeStruct((count // 2, width), jnp.bfloat16)
    return call(
        functools.partial(sum_kernel, pieces, len(totals)),
        "weighted_sums",
        FULL,
        2 * pieces * size * width * count,
        in_specs=[whole()] * (1 + len(totals))
        + [in_hbm()] * (2 * pieces - 1)
        + [in_hbm()] * len(after),
        out_specs=[whole()] * 2,
        out_shape=[sums] * 2,
        scratch_shapes=[
            pltpu.VMEM((pieces, count, size), jnp.bfloat16),
            pltpu.VMEM((pieces * size, width), jnp.bfloat16),
            pltpu.VMEM((count, width), jnp.float32),
            pltpu.SemaphoreType.DMA((pieces,)),
            pltpu.SemaphoreType.DMA((pieces,)),
        ],
    )(scale, *totals, *members, *sources, *after)


def combine_kernel(arrived_ref, *rest):
    spread_ref = rest[-1]
    planes = arrived_ref.shape[0]
    total = arrived_ref[0].astype(jnp.float32)
    for i in range(1, planes):
        total = total + arrived_ref[i].astype(jnp.float32)
    share = normalize_rows(total)
    for i in range(planes):
        spread_ref[i] = share


def combine(arrived, after):
    return call(
        combine_kernel,
        "combine",
        FULL,
        2 * arrived.size,
        in_specs=[whole()] + [pl.BlockSpec(memory_space=pl.ANY)] * len(after),
        out_specs=whole(),
        out_shape=jax.ShapeDtypeStruct(arrived.shape, arrived.dtype),
    )(arrived, *after)


def column_of(row):
    return jnp.broadcast_to(row, (8, row.shape[1])).T[:, :1]


def pack_kernel(devices, cent_count, capacity, depth_ref, raw_ref, assign_ref, table_ref, out_ref, rows, place):
    step = pl.program_id(0)
    local_rows, width = raw_ref.shape
    high_count, low_count = table_ref.shape

    @pl.when(step == 0)
    def _():
        rows[:, :width] = normalize_rows(raw_ref[...])
        cluster = assign_ref[...]
        high, low = lax.div(cluster, low_count), lax.rem(cluster, low_count)
        high_hits = lax.broadcasted_iota(jnp.int32, (high_count, local_rows), 0) == high
        by_low = lax.dot_general(
            table_ref[...].astype(jnp.bfloat16),
            jnp.where(high_hits, 1.0, 0.0).astype(jnp.bfloat16),
            (((0,), (0,)), ((), ())),
            preferred_element_type=jnp.float32,
        )
        low_hits = lax.broadcasted_iota(jnp.int32, (low_count, local_rows), 0) == low
        owner = jnp.sum(jnp.where(low_hits, by_low, 0.0), axis=0, keepdims=True).astype(jnp.int32)
        owner_hits = lax.broadcasted_iota(jnp.int32, (devices, local_rows), 0) == owner
        earlier = lax.broadcasted_iota(jnp.int32, (local_rows, local_rows), 0) < (
            lax.broadcasted_iota(jnp.int32, (local_rows, local_rows), 1)
        )
        before = jnp.dot(
            jnp.where(owner_hits, 1.0, 0.0).astype(jnp.bfloat16),
            jnp.where(earlier, 1.0, 0.0).astype(jnp.bfloat16),
            preferred_element_type=jnp.float32,
        )
        slot = jnp.sum(jnp.where(owner_hits, before, 0.0), axis=0, keepdims=True).astype(jnp.int32)
        owner_dp, owner_depth = lax.div(owner, cent_count), lax.rem(owner, cent_count)
        distance = lax.rem(owner_depth + cent_count - depth_ref[0], cent_count)
        place[...] = (owner_dp * cent_count + distance) * capacity + slot
        number = column_of((cluster + 1).astype(jnp.float32)).astype(jnp.int32)
        lane = lax.broadcasted_iota(jnp.int32, (local_rows, LABEL_LANES), 1)
        digits = jnp.where(
            lane == 0, lax.div(number, 256), jnp.where(lane == 1, lax.rem(number, 256), 0)
        )
        rows[:, width:] = digits.astype(jnp.float32).astype(jnp.bfloat16)

    size = out_ref.shape[0]
    taken = lax.broadcasted_iota(jnp.int32, (size, local_rows), 0) + step * size == place[...]
    taken = jnp.where(taken, 1.0, 0.0).astype(jnp.bfloat16)
    out_ref[...] = jnp.dot(taken, rows[...], preferred_element_type=jnp.float32).astype(jnp.bfloat16)


def pack(embeddings, assign, owner_map, depth, devices, cent_count, capacity):
    local_rows, width = embeddings.shape
    slots = devices * capacity
    tile = min(512, slots)
    low_count = 128
    return call(
        functools.partial(pack_kernel, devices, cent_count, capacity),
        "pack",
        FULL,
        2 * slots * width * local_rows,
        grid=(slots // tile,),
        in_specs=[pl.BlockSpec(memory_space=pltpu.SMEM), whole(), whole(), whole()],
        out_specs=pl.BlockSpec((tile, width + LABEL_LANES), lambda i: (i, 0)),
        out_shape=jax.ShapeDtypeStruct((slots, width + LABEL_LANES), jnp.bfloat16),
        scratch_shapes=[
            pltpu.VMEM((local_rows, width + LABEL_LANES), jnp.bfloat16),
            pltpu.VMEM((1, local_rows), jnp.int32),
        ],
    )(
        depth.reshape(1).astype(jnp.int32),
        embeddings,
        assign.reshape(1, local_rows),
        owner_map.reshape(-1, low_count).astype(jnp.float32),
    )


def join_kernel(cent_count, total_ref, label_ref, *rest):
    out_refs = rest[-(cent_count - 1) :]
    group_rows = total_ref.shape[1]
    for k in range(1, cent_count):
        out_refs[k - 1][:, :group_rows] = total_ref[...]
        out_refs[k - 1][:, group_rows:] = label_ref[cent_count - k : cent_count - k + 1]


def join(totals, label, after):
    cent_count, labels = label.shape
    joined = jax.ShapeDtypeStruct((1, totals.shape[1] + labels), jnp.float32)
    return call(
        functools.partial(join_kernel, cent_count),
        "join",
        FULL,
        totals.size,
        in_specs=[whole()] * 2 + [in_hbm()] * len(after),
        out_specs=[whole()] * (cent_count - 1),
        out_shape=[joined] * (cent_count - 1),
    )(totals, label, *after)


def similarity_kernel(cent_count, depth_ref, *rest):
    block_refs = rest[:cent_count]
    row_ref, out_ref, gathered, column, sem = rest[cent_count:]
    step = pl.program_id(0)

    @pl.when(step == 0)
    def _():
        arriving = []
        for k in range(cent_count):
            source = lax.rem(depth_ref[0] + cent_count - k, cent_count)
            block = block_refs[k].at[:, 0, :, pl.ds(0, gathered.shape[-1])] if k == 0 else block_refs[k]
            arriving.append(pltpu.make_async_copy(block, gathered.at[:, source], sem.at[k]))
            arriving[-1].start()
        row = row_ref[...]
        column[...] = column_of(jnp.where(row > 0.0, row, -1.0))
        for copy in arriving:
            copy.wait()

    size = out_ref.shape[1]
    slots, width = out_ref.shape[2], gathered.shape[-1]
    per_step = size // (gathered.shape[1] * gathered.shape[2])
    rows = gathered[pl.ds(step * per_step, per_step)].reshape(size, width)
    inner = contract_final_axis(rows, gathered[...].reshape(slots, width))
    start = pl.multiple_of(step * size, size)
    same = column[pl.ds(start, size)] == row_ref[...]
    out_ref[0] = jnp.where(same, inner * math.sqrt(width), 0.0).astype(jnp.bfloat16)
    main_diagonal = lax.broadcasted_iota(jnp.int32, (size, size), 0) == (
        lax.broadcasted_iota(jnp.int32, (size, size), 1)
    )
    corner = out_ref[0, :, pl.ds(start, size)]
    out_ref[0, :, pl.ds(start, size)] = jnp.where(
        main_diagonal, 0.0, corner.astype(jnp.float32)
    ).astype(jnp.bfloat16)


def similarity_of(blocks, label, depth):
    cent_count = len(blocks)
    dp_count, capacity, width = blocks[1].shape
    slots = cent_count * dp_count * capacity
    tile = min(256, slots)
    return call(
        functools.partial(similarity_kernel, cent_count),
        "similarity",
        FULL,
        2 * slots * slots * width,
        grid=(slots // tile,),
        in_specs=[pl.BlockSpec(memory_space=pltpu.SMEM)]
        + [in_hbm()] * cent_count
        + [pl.BlockSpec((1, slots), lambda i: (0, 0))],
        out_specs=pl.BlockSpec((1, tile, slots), lambda i: (0, i, 0)),
        out_shape=jax.ShapeDtypeStruct((1, slots, slots), jnp.bfloat16),
        scratch_shapes=[
            pltpu.VMEM((dp_count, cent_count, capacity, width), jnp.bfloat16),
            pltpu.VMEM((slots, 1), jnp.float32),
            pltpu.SemaphoreType.DMA((cent_count,)),
        ],
    )(depth.reshape(1).astype(jnp.int32), *blocks, label)


def shards(embeddings, init_centroids, assign, owner_map):
    devices = lax.axis_size(AXES)
    cent_count = lax.axis_size("cent")
    dp_count = lax.axis_size("dp")
    depth = lax.axis_index("cent")
    local_rows, feature_width = embeddings.shape
    planes = dp_count // 2
    core = lax.axis_index("dp") % 2
    half = init_centroids.shape[0] // 2
    share = half // planes
    capacity = 2 * local_rows // devices
    group_rows = cent_count * local_rows

    def send(value, step):
        return lax.ppermute(
            value, "cent", [(z, (z + step) % cent_count) for z in range(cent_count)]
        )

    def exchange(value):
        return lax.all_to_all(value, "dp", 0, 0, tiled=True)

    same_core = [[2 * chip + c for chip in range(planes)] for c in range(2)]
    other_core = [(i, i + 1 - 2 * (i % 2)) for i in range(dp_count)]

    def exchange_plane(value):
        return lax.all_to_all(value, "dp", 0, 0, axis_index_groups=same_core, tiled=True)

    def swap_cores(value):
        return lax.ppermute(value, "dp", other_core)

    cut = local_rows // 2
    first, second = embeddings[:cut], embeddings[cut:]
    below_first, above_second = send(first, 1), send(second, -1)
    below_second, above_first = send(second, 1), send(first, -1)
    far_first, far_second = send(below_first, 1), send(above_second, -1)
    received = [above_first, above_second, far_first, far_second, below_first, below_second]
    sources = [embeddings] + received

    packed = pack(embeddings, assign, owner_map, depth, devices, cent_count, capacity)
    routed = exchange(packed.reshape(dp_count, cent_count * capacity, -1)).reshape(
        dp_count, cent_count, capacity, -1
    )
    digits = routed[..., feature_width : feature_width + 2].astype(jnp.float32)
    routed_label = (
        (digits[..., 0] * 256.0 + digits[..., 1])
        .transpose(1, 0, 2)
        .reshape(cent_count, dp_count * capacity)
    )

    initial = normalize_rows(init_centroids)
    own_half = lax.dynamic_slice_in_dim(initial, core * half, half, 0)
    other_half = lax.dynamic_slice_in_dim(initial, (1 - core) * half, half, 0)
    block = jnp.concatenate([own_half, other_half])
    scored = [
        score_piece(piece, block, FAR_COST if piece is far_first or piece is far_second else NEAR_COST)
        for piece in [first, second] + received
    ]
    members = [member for member, _, _ in scored]
    partial_total = jnp.concatenate([total for _, total, _ in scored], axis=1)
    scale = jnp.concatenate([scale for _, _, scale in scored], axis=1)

    def reduced(members, totals, after):
        own, for_sibling = weighted_sums(members, sources, scale, totals, after)
        both = own.astype(jnp.float32) + swap_cores(for_sibling).astype(jnp.float32)
        return exchange_plane(both.astype(jnp.bfloat16).reshape(planes, share, feature_width))

    totals = [partial_total] + [send(partial_total, -k) for k in range(1, cent_count)]
    arrived = reduced(members, totals, [routed])

    parted = [routed[:, k, :, :feature_width] for k in range(cent_count)]
    blocks = [routed, send(parted[1], 1), None, send(parted[3], -1)]
    blocks[2] = send(parted[2] + blocks[1] * 0, 2)

    own_half = exchange_plane(combine(arrived, [blocks[1], blocks[3]])).reshape(half, feature_width)
    members, partial_total = score_rows(sources, scale, own_half, swap_cores(own_half))
    joined = join(partial_total, routed_label, [blocks[2]])
    totals, label = [partial_total], [routed_label[0].reshape(dp_count, capacity)]
    for k in range(1, cent_count):
        got = send(joined[k - 1], -k)
        totals.append(got)
        label.append(got[:, group_rows:].reshape(dp_count, capacity))
    label = jnp.roll(jnp.stack(label, axis=1), depth, axis=1).reshape(1, -1)
    similarity = similarity_of(blocks, label, depth)
    arrived = reduced(members, totals, [])
    own_half = exchange_plane(combine(arrived, [similarity])).reshape(half, feature_width)
    other_half = swap_cores(own_half)
    centroids = jnp.where(
        core == 0,
        jnp.concatenate([own_half, other_half]),
        jnp.concatenate([other_half, own_half]),
    ).astype(jnp.float32) * math.sqrt(feature_width)
    return (centroids, similarity)


def solution(mesh):
    return jax.shard_map(
        shards,
        mesh=mesh,
        in_specs=(P(AXES, None), P("cent", None), P(AXES), P()),
        out_specs=(P("cent", None), P(AXES, None, None)),
        check_vma=False,
    )
```

```python
import functools
import math

import jax
import jax.numpy as jnp
from jax import lax
from jax.experimental import pallas as pl
from jax.experimental.pallas import tpu as pltpu
from jax.sharding import PartitionSpec as P

ROUNDS = 2
AXES = ("dp", "cent")

epsilon = 1e-06
logit_divisor = 0.02
MIB = 1024 * 1024
LABEL_LANES = 128
NEAR_COST = 1_000_000
OWN_COST = 6_000_000_000
FAR_COST = 25_000_000_000
FULL = 61


def unit(matrix):
    wide = matrix.astype(jnp.float32)
    return wide * (1.0 / jnp.sqrt(jnp.sum(wide * wide, axis=-1, keepdims=True) + epsilon))


def normalize_rows(matrix):
    return unit(matrix).astype(jnp.bfloat16)


def contract_final_axis(left, right):
    return lax.dot_general(
        left, right, (((1,), (1,)), ((), ())), preferred_element_type=jnp.float32
    )


def whole():
    return pl.BlockSpec(memory_space=pltpu.VMEM)


def in_hbm():
    return pl.BlockSpec(memory_space=pl.ANY)


def call(kernel, name, vmem, flops, **options):
    return pl.pallas_call(
        kernel,
        name=name,
        cost_estimate=pl.CostEstimate(flops=int(flops), bytes_accessed=1 << 20, transcendentals=0),
        compiler_params=pltpu.CompilerParams(vmem_limit_bytes=vmem * MIB),
        **options,
    )


def membership_of(block, rows, scale):
    scores = contract_final_axis(block, rows)
    membership = jnp.exp2(scores * (scale * (math.log2(math.e) / logit_divisor)))
    return membership.astype(jnp.bfloat16), jnp.sum(membership, axis=0, keepdims=True)


def piece_kernel(raw_ref, block_ref, *rest):
    *member_refs, total_ref, scale_ref = rest
    wide = raw_ref[...].astype(jnp.float32)
    squares = jnp.sum(wide * wide, axis=-1, keepdims=True) + epsilon
    scale = (1.0 / jnp.sqrt(jnp.broadcast_to(squares, (squares.shape[0], 8)))).T[:1]
    scale_ref[...] = scale
    size = raw_ref.shape[0] // len(member_refs)
    for i, member_ref in enumerate(member_refs):
        at = slice(i * size, (i + 1) * size)
        member_ref[...], total_ref[:, at] = membership_of(block_ref[...], raw_ref[at], scale[:, at])


def score_piece(raw, block, pieces, cost):
    size, width = raw.shape
    count = block.shape[0]
    line = jax.ShapeDtypeStruct((1, size), jnp.float32)
    return call(
        piece_kernel,
        "score_piece",
        12,
        cost,
        in_specs=[whole(), whole()],
        out_specs=[whole()] * (pieces + 2),
        out_shape=[jax.ShapeDtypeStruct((count, size // pieces), jnp.bfloat16)] * pieces + [line] * 2,
    )(raw, block)


def fetches(sources, taken, sems):
    size = sources[1].shape[0]
    parts = [sources[0].at[pl.ds(0, size)], sources[0].at[pl.ds(size, size)]] + list(sources[1:])
    return [
        pltpu.make_async_copy(part, taken.at[pl.ds(i * size, size)], sems.at[i])
        for i, part in enumerate(parts)
    ]


def score_kernel(pieces, scale_ref, own_ref, other_ref, *rest):
    sources, outs = rest[: pieces - 1], rest[pieces - 1 :]
    member_refs, total_ref = outs[:pieces], outs[pieces]
    taken, members, block, in_sem, out_sem = outs[pieces + 1 :]
    half = own_ref.shape[0]
    size = sources[1].shape[0]
    arriving = fetches(sources, taken, in_sem)
    for copy in arriving:
        copy.start()
    block[:half], block[half:] = own_ref[...], other_ref[...]
    leaving = []
    for i in range(pieces):
        arriving[i].wait()
        at = slice(i * size, (i + 1) * size)
        members[i], total_ref[:, at] = membership_of(block[...], taken[at], scale_ref[:, at])
        leaving.append(pltpu.make_async_copy(members.at[i], member_refs[i], out_sem.at[i]))
        leaving[-1].start()
    for copy in leaving:
        copy.wait()


def score_rows(sources, scale, own_half, other_half):
    pieces = len(sources) + 1
    size, width = sources[1].shape
    count = 2 * own_half.shape[0]
    each = pltpu.SemaphoreType.DMA((pieces,))
    out = call(
        functools.partial(score_kernel, pieces),
        "score_rows",
        FULL,
        NEAR_COST,
        in_specs=[whole()] * 3 + [in_hbm()] * len(sources),
        out_specs=[in_hbm()] * pieces + [whole()],
        out_shape=[jax.ShapeDtypeStruct((count, size), jnp.bfloat16)] * pieces
        + [jax.ShapeDtypeStruct((1, pieces * size), jnp.float32)],
        scratch_shapes=[
            pltpu.VMEM((pieces * size, width), jnp.bfloat16),
            pltpu.VMEM((pieces, count, size), jnp.bfloat16),
            pltpu.VMEM((count, width), jnp.bfloat16),
            each,
            each,
        ],
    )(scale, own_half, other_half, *sources)
    return out[:pieces], out[pieces]


def sum_kernel(pieces, depth, core_ref, scale_ref, *rest):
    total_refs, rest = rest[:depth], rest[depth:]
    member_refs, sources = rest[:pieces], rest[pieces : 2 * pieces - 1]
    sums_ref, members, taken, running, member_sem, row_sem = rest[-6:]
    half = running.shape[0] // 2
    size = sources[1].shape[0]
    arriving = [
        (rows, pltpu.make_async_copy(member_refs[i], members.at[i], member_sem.at[i]))
        for i, rows in enumerate(fetches(sources, taken, row_sem))
    ]
    for pair in arriving:
        for copy in pair:
            copy.start()
    for i in range(pieces):
        for copy in arriving[i]:
            copy.wait()
        at = slice(i * size, (i + 1) * size)
        total = total_refs[0][:, at]
        for k in range(1, depth):
            j = (i + pieces - k * (pieces // depth)) % pieces
            total = total + total_refs[k][:, j * size : (j + 1) * size]
        weights = members[i].astype(jnp.float32) * (scale_ref[:, at] / total)
        product = jnp.dot(
            weights.astype(jnp.bfloat16), taken[at], preferred_element_type=jnp.float32
        )
        if i == 0:
            running[...] = product
        else:
            running[...] += product
    own, other = running[:half].astype(jnp.bfloat16), running[half:].astype(jnp.bfloat16)
    chips, _, share, width = sums_ref.shape
    sums_ref[:, core_ref[0]] = own.reshape(chips, share, width)
    sums_ref[:, 1 - core_ref[0]] = other.reshape(chips, share, width)


def weighted_sums(members, sources, scale, totals, core, chips, after):
    pieces = len(members)
    count, size = members[0].shape
    width = sources[0].shape[1]
    return call(
        functools.partial(sum_kernel, pieces, len(totals)),
        "weighted_sums",
        FULL,
        2 * pieces * size * width * count,
        in_specs=[pl.BlockSpec(memory_space=pltpu.SMEM)]
        + [whole()] * (1 + len(totals))
        + [in_hbm()] * (2 * pieces - 1)
        + [in_hbm()] * len(after),
        out_specs=whole(),
        out_shape=jax.ShapeDtypeStruct((chips, 2, count // 2 // chips, width), jnp.bfloat16),
        scratch_shapes=[
            pltpu.VMEM((pieces, count, size), jnp.bfloat16),
            pltpu.VMEM((pieces * size, width), jnp.bfloat16),
            pltpu.VMEM((count, width), jnp.float32),
            pltpu.SemaphoreType.DMA((pieces,)),
            pltpu.SemaphoreType.DMA((pieces,)),
        ],
    )(core.reshape(1).astype(jnp.int32), scale, *totals, *members, *sources, *after)


def combine_kernel(arrived_ref, *rest):
    spread_ref = rest[-1]
    total = arrived_ref[0].astype(jnp.float32)
    for i in range(1, arrived_ref.shape[0]):
        total = total + arrived_ref[i].astype(jnp.float32)
    share = normalize_rows(total)
    for i in range(spread_ref.shape[0]):
        spread_ref[i] = share


def combine(arrived, receivers, after):
    return call(
        combine_kernel,
        "combine",
        8,
        2 * arrived.size,
        in_specs=[whole()] + [in_hbm()] * len(after),
        out_specs=whole(),
        out_shape=jax.ShapeDtypeStruct((receivers,) + arrived.shape[1:], arrived.dtype),
    )(arrived, *after)


def finish_kernel(core_ref, own_ref, other_ref, out_ref):
    half, width = own_ref.shape
    core = core_ref[0]
    for side, ref in ((core, own_ref), (1 - core, other_ref)):
        at = pl.ds(pl.multiple_of(side * half, half), half)
        out_ref[at] = ref[...].astype(jnp.float32) * math.sqrt(width)


def finish(own_half, other_half, core):
    half, width = own_half.shape
    return call(
        finish_kernel,
        "finish",
        8,
        own_half.size,
        in_specs=[pl.BlockSpec(memory_space=pltpu.SMEM), whole(), whole()],
        out_specs=whole(),
        out_shape=jax.ShapeDtypeStruct((2 * half, width), jnp.float32),
    )(core.reshape(1).astype(jnp.int32), own_half, other_half)


def pack_kernel(devices, cent_count, capacity, depth_ref, raw_ref, assign_ref, table_ref, out_ref, rows, place):
    step = pl.program_id(0)
    local_rows, width = raw_ref.shape
    high_count, low_count = table_ref.shape

    @pl.when(step == 0)
    def _():
        rows[:, :width] = normalize_rows(raw_ref[...])
        cluster = assign_ref[...]
        high, low = lax.div(cluster, low_count), lax.rem(cluster, low_count)
        high_hits = lax.broadcasted_iota(jnp.int32, (high_count, local_rows), 0) == high
        by_low = lax.dot_general(
            table_ref[...].astype(jnp.bfloat16),
            jnp.where(high_hits, 1.0, 0.0).astype(jnp.bfloat16),
            (((0,), (0,)), ((), ())),
            preferred_element_type=jnp.float32,
        )
        low_hits = lax.broadcasted_iota(jnp.int32, (low_count, local_rows), 0) == low
        owner = jnp.sum(jnp.where(low_hits, by_low, 0.0), axis=0, keepdims=True).astype(jnp.int32)
        owner_hits = lax.broadcasted_iota(jnp.int32, (devices, local_rows), 0) == owner
        group = min(128, local_rows)
        earlier = lax.broadcasted_iota(jnp.int32, (group, group), 0) < (
            lax.broadcasted_iota(jnp.int32, (group, group), 1)
        )
        earlier = jnp.where(earlier, 1.0, 0.0).astype(jnp.bfloat16)
        ones = jnp.where(owner_hits, 1.0, 0.0)
        before, seen = [], jnp.zeros((devices, 1), jnp.float32)
        for at in range(0, local_rows, group):
            some = ones[:, at : at + group]
            before.append(
                jnp.dot(some.astype(jnp.bfloat16), earlier, preferred_element_type=jnp.float32) + seen
            )
            seen = seen + jnp.sum(some, axis=1, keepdims=True)
        before = jnp.concatenate(before, axis=1)
        slot = jnp.sum(jnp.where(owner_hits, before, 0.0), axis=0, keepdims=True).astype(jnp.int32)
        owner_dp, owner_depth = lax.div(owner, cent_count), lax.rem(owner, cent_count)
        distance = lax.rem(owner_depth + cent_count - depth_ref[0], cent_count)
        place[...] = (owner_dp * cent_count + distance) * capacity + slot
        number = cluster + 1
        lane = lax.broadcasted_iota(jnp.int32, (LABEL_LANES, local_rows), 0)
        digits = jnp.where(
            lane == 0, lax.div(number, 256), jnp.where(lane == 1, lax.rem(number, 256), 0)
        )
        rows[:, width:] = digits.astype(jnp.float32).T.astype(jnp.bfloat16)

    size = out_ref.shape[0]
    taken = lax.broadcasted_iota(jnp.int32, (size, local_rows), 0) + step * size == place[...]
    taken = jnp.where(taken, 1.0, 0.0).astype(jnp.bfloat16)
    out_ref[...] = jnp.dot(taken, rows[...], preferred_element_type=jnp.float32).astype(jnp.bfloat16)


def pack(embeddings, assign, owner_map, depth, devices, cent_count, capacity):
    local_rows, width = embeddings.shape
    slots = devices * capacity
    tile = min(512, slots)
    low_count = 128
    return call(
        functools.partial(pack_kernel, devices, cent_count, capacity),
        "pack",
        FULL,
        2 * slots * width * local_rows,
        grid=(slots // tile,),
        in_specs=[pl.BlockSpec(memory_space=pltpu.SMEM), whole(), whole(), whole()],
        out_specs=pl.BlockSpec((tile, width + LABEL_LANES), lambda i: (i, 0)),
        out_shape=jax.ShapeDtypeStruct((slots, width + LABEL_LANES), jnp.bfloat16),
        scratch_shapes=[
            pltpu.VMEM((local_rows, width + LABEL_LANES), jnp.bfloat16),
            pltpu.VMEM((1, local_rows), jnp.int32),
        ],
    )(
        depth.reshape(1).astype(jnp.int32),
        embeddings,
        assign.reshape(1, local_rows),
        owner_map.reshape(-1, low_count).astype(jnp.float32),
    )


def order_kernel(*refs):
    del refs


def order(value, after):
    return call(
        order_kernel,
        "order",
        FULL,
        1,
        in_specs=[in_hbm()] * (1 + len(after)),
        out_specs=in_hbm(),
        out_shape=jax.ShapeDtypeStruct(value.shape, value.dtype),
        input_output_aliases={0: 0},
    )(value, *after)


def hold_kernel(value_ref, *rest):
    rest[-1][...] = value_ref[...]


def hold(value, after):
    return call(
        hold_kernel,
        "hold",
        8,
        value.size,
        in_specs=[whole()] + [in_hbm()] * len(after),
        out_specs=whole(),
        out_shape=jax.ShapeDtypeStruct(value.shape, value.dtype),
    )(value, *after)


def similarity_kernel(cent_count, first, depth_ref, *rest):
    block_refs = rest[:cent_count]
    out_ref, flag_ref, gathered, column, row, sem = rest[-6:]
    step = pl.program_id(0)
    dp_count, _, capacity, lanes = gathered.shape
    size, slots = out_ref.shape[1:]
    width = lanes - LABEL_LANES

    @pl.when(step == 0)
    def _():
        arriving = []
        for k in range(cent_count):
            source = lax.rem(depth_ref[0] + cent_count - k, cent_count)
            block = block_refs[k].at[:, 0] if k == 0 else block_refs[k]
            arriving.append(pltpu.make_async_copy(block, gathered.at[:, source], sem.at[k]))
            arriving[-1].start()
        for copy in arriving:
            copy.wait()
        digits = gathered[:, :, :, width:].reshape(slots, LABEL_LANES).astype(jnp.float32)
        number = digits[:, 0:1] * 256.0 + digits[:, 1:2]
        column[...] = jnp.where(number > 0.0, number, -1.0)
        across = digits.T
        row[...] = across[0:1] * 256.0 + across[1:2]
        flag_ref[...] = jnp.zeros_like(flag_ref)

    per_step = size // (cent_count * capacity)
    start = pl.multiple_of((first + step) * size, size)
    rows = gathered[pl.ds((first + step) * per_step, per_step), :, :, :width].reshape(size, width)
    every = gathered[:, :, :, :width].reshape(slots, width)
    same = column[pl.ds(start, size)] == row[...]
    out_ref[0] = jnp.where(
        same, contract_final_axis(rows, every) * math.sqrt(width), 0.0
    ).astype(jnp.bfloat16)
    main_diagonal = lax.broadcasted_iota(jnp.int32, (size, size), 0) == (
        lax.broadcasted_iota(jnp.int32, (size, size), 1)
    )
    corner = out_ref[0, :, pl.ds(start, size)]
    out_ref[0, :, pl.ds(start, size)] = jnp.where(
        main_diagonal, 0.0, corner.astype(jnp.float32)
    ).astype(jnp.bfloat16)


def similarity_of(blocks, depth, part, parts, held):
    cent_count = len(blocks)
    dp_count, capacity, lanes = blocks[1].shape
    slots = cent_count * dp_count * capacity
    tile = min(256, slots // parts)
    steps = slots // tile // parts
    aliased = [] if held is None else [held]
    return call(
        functools.partial(similarity_kernel, cent_count, part * steps),
        "similarity",
        FULL,
        2 * slots * slots * lanes // parts,
        grid=(steps,),
        in_specs=[pl.BlockSpec(memory_space=pltpu.SMEM)] + [in_hbm()] * (cent_count + len(aliased)),
        out_specs=[
            pl.BlockSpec((1, tile, slots), lambda i: (0, part * steps + i, 0)),
            pl.BlockSpec((8, 128), lambda i: (0, 0)),
        ],
        out_shape=[
            jax.ShapeDtypeStruct((1, slots, slots), jnp.bfloat16),
            jax.ShapeDtypeStruct((8, 128), jnp.float32),
        ],
        scratch_shapes=[
            pltpu.VMEM((dp_count, cent_count, capacity, lanes), jnp.bfloat16),
            pltpu.VMEM((slots, 1), jnp.float32),
            pltpu.VMEM((1, slots), jnp.float32),
            pltpu.SemaphoreType.DMA((cent_count,)),
        ],
        input_output_aliases={1 + cent_count: 0} if aliased else {},
    )(depth.reshape(1).astype(jnp.int32), *blocks, *aliased)


def shards(embeddings, init_centroids, assign, owner_map):
    devices = lax.axis_size(AXES)
    cent_count = lax.axis_size("cent")
    dp_count = lax.axis_size("dp")
    depth = lax.axis_index("cent")
    local_rows, feature_width = embeddings.shape
    planes = dp_count // 2
    core = lax.axis_index("dp") % 2
    half = init_centroids.shape[0] // 2
    share = half // planes
    capacity = 2 * local_rows // devices
    group_rows = cent_count * local_rows

    def send(value, step):
        return lax.ppermute(
            value, "cent", [(z, (z + step) % cent_count) for z in range(cent_count)]
        )

    def exchange(value):
        return lax.all_to_all(value, "dp", 0, 0, tiled=True)

    same_core = [[2 * chip + c for chip in range(planes)] for c in range(2)]
    other_core = [(i, i + 1 - 2 * (i % 2)) for i in range(dp_count)]

    def exchange_plane(value):
        return lax.all_to_all(value, "dp", 0, 0, axis_index_groups=same_core, tiled=True)

    def swap_cores(value):
        return lax.ppermute(value, "dp", other_core)

    cut = local_rows // 2
    first, second = embeddings[:cut], embeddings[cut:]
    below_first, above_second = send(first, 1), send(second, -1)
    below_second, above_first = send(second, 1), send(first, -1)
    far_first, far_second = send(below_first, 1), send(above_second, -1)
    received = [above_first, above_second, far_first, far_second, below_first, below_second]
    sources = [embeddings] + received

    packed = pack(embeddings, assign, owner_map, depth, devices, cent_count, capacity)
    routed = exchange(packed.reshape(dp_count, cent_count * capacity, -1)).reshape(
        dp_count, cent_count, capacity, -1
    )
    initial = normalize_rows(init_centroids)
    own_half = lax.dynamic_slice_in_dim(initial, core * half, half, 0)
    other_half = lax.dynamic_slice_in_dim(initial, (1 - core) * half, half, 0)
    block = jnp.concatenate([own_half, other_half])
    scored = [score_piece(embeddings, block, 2, OWN_COST)] + [
        score_piece(piece, block, 1, FAR_COST if piece is far_first or piece is far_second else NEAR_COST)
        for piece in received
    ]
    members = [member for *parts, _, _ in scored for member in parts]
    partial_total = jnp.concatenate([total for *_, total, _ in scored], axis=1)
    scale = jnp.concatenate([scale for *_, scale in scored], axis=1)

    totals = [partial_total] + [send(partial_total, -k) for k in range(1, cent_count)]
    parted = [routed[:, k] for k in range(cent_count)]
    sums = weighted_sums(members, sources, scale, totals, core, planes, parted[1:])
    arrived = exchange(sums.reshape(dp_count, share, feature_width))

    blocks = [routed, send(parted[1], 1), None, send(parted[3], -1)]
    blocks[2] = send(order(parted[2], [blocks[1], blocks[3]]), 2)

    own_half = exchange_plane(combine(arrived, planes, [])).reshape(half, feature_width)
    members, partial_total = score_rows(sources, scale, own_half, swap_cores(own_half))
    totals = [partial_total] + [send(partial_total, -k) for k in range(1, cent_count)]
    sums = weighted_sums(members, sources, scale, totals, core, planes, [blocks[2]])
    arrived = exchange(sums.reshape(dp_count, share, feature_width))
    similarity, upper = similarity_of(blocks, depth, 0, 2, None)
    spread = combine(arrived, planes, [upper])
    similarity, lower = similarity_of(blocks, depth, 1, 2, similarity)
    own_half = hold(exchange_plane(spread).reshape(half, feature_width), [lower])
    return (finish(own_half, swap_cores(own_half), core), similarity)


def solution(mesh):
    return jax.shard_map(
        shards,
        mesh=mesh,
        in_specs=(P(AXES, None), P("cent", None), P(AXES), P()),
        out_specs=(P("cent", None), P(AXES, None, None)),
        check_vma=False,
    )
```

```python
import functools
import math

import jax
import jax.numpy as jnp
from jax import lax
from jax.experimental import pallas as pl
from jax.experimental.pallas import tpu as pltpu
from jax.sharding import PartitionSpec as P

ROUNDS = 2
AXES = ("dp", "cent")

epsilon = 1e-06
logit_divisor = 0.02
MIB = 1024 * 1024
LABEL_LANES = 128
NEAR_COST = 1_000_000
OWN_COST = 6_000_000_000
FAR_COST = 50_000_000_000
FULL = 61


def unit(matrix):
    wide = matrix.astype(jnp.float32)
    return wide * (1.0 / jnp.sqrt(jnp.sum(wide * wide, axis=-1, keepdims=True) + epsilon))


def normalize_rows(matrix):
    return unit(matrix).astype(jnp.bfloat16)


def contract_final_axis(left, right):
    return lax.dot_general(
        left, right, (((1,), (1,)), ((), ())), preferred_element_type=jnp.float32
    )


def whole():
    return pl.BlockSpec(memory_space=pltpu.VMEM)


def in_hbm():
    return pl.BlockSpec(memory_space=pl.ANY)


def call(kernel, name, vmem, flops, **options):
    return pl.pallas_call(
        kernel,
        name=name,
        cost_estimate=pl.CostEstimate(flops=int(flops), bytes_accessed=1 << 20, transcendentals=0),
        compiler_params=pltpu.CompilerParams(vmem_limit_bytes=vmem * MIB),
        **options,
    )


def membership_of(block, rows, scale):
    scores = contract_final_axis(block, rows)
    membership = jnp.exp2(scores * (scale * (math.log2(math.e) / logit_divisor)))
    return membership.astype(jnp.bfloat16), jnp.sum(membership, axis=0, keepdims=True)


def piece_kernel(sources, block_ref, *rest):
    raw_refs, member_refs = rest[:sources], rest[sources:-2]
    total_ref, scale_ref = rest[-2:]
    size = member_refs[0].shape[1]
    parts = [(ref, at) for ref in raw_refs for at in range(0, ref.shape[0], size)]
    for i, (ref, start) in enumerate(parts):
        raw = ref[start : start + size]
        at = slice(i * size, (i + 1) * size)
        wide = raw.astype(jnp.float32)
        squares = jnp.sum(wide * wide, axis=-1, keepdims=True) + epsilon
        scale = (1.0 / jnp.sqrt(jnp.broadcast_to(squares, (size, 8)))).T[:1]
        scale_ref[:, at] = scale
        member_refs[i][...], total_ref[:, at] = membership_of(block_ref[...], raw, scale)


def score_piece(raws, block, size, cost):
    rows = sum(raw.shape[0] for raw in raws)
    count = block.shape[0]
    line = jax.ShapeDtypeStruct((1, rows), jnp.float32)
    pieces = rows // size
    return call(
        functools.partial(piece_kernel, len(raws)),
        "score_piece",
        12,
        cost,
        in_specs=[whole()] * (1 + len(raws)),
        out_specs=[whole()] * (pieces + 2),
        out_shape=[jax.ShapeDtypeStruct((count, size), jnp.bfloat16)] * pieces + [line] * 2,
    )(block, *raws)


def fetches(sources, size, taken, sems):
    parts = [
        source.at[pl.ds(at, size)] for source in sources for at in range(0, source.shape[0], size)
    ]
    return [
        pltpu.make_async_copy(part, taken.at[pl.ds(i * size, size)], sems.at[i])
        for i, part in enumerate(parts)
    ]


def score_kernel(pieces, scale_ref, own_ref, other_ref, *rest):
    *sources, total_ref, taken, members, block, in_sem, out_sem = rest
    sources, member_refs = sources[:-pieces], sources[-pieces:]
    half = own_ref.shape[0]
    size = members.shape[2]
    arriving = fetches(sources, size, taken, in_sem)
    for copy in arriving:
        copy.start()
    block[:half], block[half:] = own_ref[...], other_ref[...]
    leaving = []
    for i in range(pieces):
        arriving[i].wait()
        at = slice(i * size, (i + 1) * size)
        members[i], total_ref[:, at] = membership_of(block[...], taken[at], scale_ref[:, at])
        leaving.append(pltpu.make_async_copy(members.at[i], member_refs[i], out_sem.at[i]))
        leaving[-1].start()
    for copy in leaving:
        copy.wait()


def score_rows(sources, scale, own_half, other_half, size):
    pieces = scale.shape[1] // size
    width = sources[0].shape[1]
    count = 2 * own_half.shape[0]
    each = pltpu.SemaphoreType.DMA((pieces,))
    out = call(
        functools.partial(score_kernel, pieces),
        "score_rows",
        FULL,
        NEAR_COST,
        in_specs=[whole()] * 3 + [in_hbm()] * len(sources),
        out_specs=[in_hbm()] * pieces + [whole()],
        out_shape=[jax.ShapeDtypeStruct((count, size), jnp.bfloat16)] * pieces
        + [jax.ShapeDtypeStruct((1, pieces * size), jnp.float32)],
        scratch_shapes=[
            pltpu.VMEM((pieces * size, width), jnp.bfloat16),
            pltpu.VMEM((pieces, count, size), jnp.bfloat16),
            pltpu.VMEM((count, width), jnp.bfloat16),
            each,
            each,
        ],
    )(scale, own_half, other_half, *sources)
    return out[:pieces], out[pieces]


def sum_kernel(pieces, depth, source_count, core_ref, scale_ref, *rest):
    total_refs, rest = rest[:depth], rest[depth:]
    sums_ref, members, taken, running, member_sem, row_sem = rest[-6:]
    member_refs, sources = rest[:pieces], rest[pieces : pieces + source_count]
    half = running.shape[0] // 2
    size = members.shape[2]
    arriving = [
        (rows, pltpu.make_async_copy(member_refs[i], members.at[i], member_sem.at[i]))
        for i, rows in enumerate(fetches(sources, size, taken, row_sem))
    ]
    for pair in arriving:
        for copy in pair:
            copy.start()
    for i in range(pieces):
        for copy in arriving[i]:
            copy.wait()
        at = slice(i * size, (i + 1) * size)
        total = total_refs[0][:, at]
        for k in range(1, depth):
            j = (i + pieces - k * (pieces // depth)) % pieces
            total = total + total_refs[k][:, j * size : (j + 1) * size]
        weights = members[i].astype(jnp.float32) * (scale_ref[:, at] / total)
        product = jnp.dot(
            weights.astype(jnp.bfloat16), taken[at], preferred_element_type=jnp.float32
        )
        if i == 0:
            running[...] = product
        else:
            running[...] += product
    own, other = running[:half].astype(jnp.bfloat16), running[half:].astype(jnp.bfloat16)
    chips, _, share, width = sums_ref.shape
    sums_ref[:, core_ref[0]] = own.reshape(chips, share, width)
    sums_ref[:, 1 - core_ref[0]] = other.reshape(chips, share, width)


def weighted_sums(members, sources, scale, totals, core, chips, after):
    pieces = len(members)
    count, size = members[0].shape
    width = sources[0].shape[1]
    return call(
        functools.partial(sum_kernel, pieces, len(totals), len(sources)),
        "weighted_sums",
        FULL,
        2 * pieces * size * width * count,
        in_specs=[pl.BlockSpec(memory_space=pltpu.SMEM)]
        + [whole()] * (1 + len(totals))
        + [in_hbm()] * (pieces + len(sources))
        + [in_hbm()] * len(after),
        out_specs=whole(),
        out_shape=jax.ShapeDtypeStruct((chips, 2, count // 2 // chips, width), jnp.bfloat16),
        scratch_shapes=[
            pltpu.VMEM((pieces, count, size), jnp.bfloat16),
            pltpu.VMEM((pieces * size, width), jnp.bfloat16),
            pltpu.VMEM((count, width), jnp.float32),
            pltpu.SemaphoreType.DMA((pieces,)),
            pltpu.SemaphoreType.DMA((pieces,)),
        ],
    )(core.reshape(1).astype(jnp.int32), scale, *totals, *members, *sources, *after)


def combine_kernel(arrived_ref, *rest):
    spread_ref = rest[-1]
    total = arrived_ref[0].astype(jnp.float32)
    for i in range(1, arrived_ref.shape[0]):
        total = total + arrived_ref[i].astype(jnp.float32)
    share = normalize_rows(total)
    for i in range(spread_ref.shape[0]):
        spread_ref[i] = share


def combine(arrived, receivers, after):
    return call(
        combine_kernel,
        "combine",
        8,
        2 * arrived.size,
        in_specs=[whole()] + [in_hbm()] * len(after),
        out_specs=whole(),
        out_shape=jax.ShapeDtypeStruct((receivers,) + arrived.shape[1:], arrived.dtype),
    )(arrived, *after)


def finish_kernel(core_ref, own_ref, other_ref, out_ref):
    half, width = own_ref.shape
    core = core_ref[0]
    for side, ref in ((core, own_ref), (1 - core, other_ref)):
        at = pl.ds(pl.multiple_of(side * half, half), half)
        out_ref[at] = ref[...].astype(jnp.float32) * math.sqrt(width)


def finish(own_half, other_half, core):
    half, width = own_half.shape
    return call(
        finish_kernel,
        "finish",
        8,
        own_half.size,
        in_specs=[pl.BlockSpec(memory_space=pltpu.SMEM), whole(), whole()],
        out_specs=whole(),
        out_shape=jax.ShapeDtypeStruct((2 * half, width), jnp.float32),
    )(core.reshape(1).astype(jnp.int32), own_half, other_half)


def pack_kernel(devices, cent_count, capacity, depth_ref, raw_ref, assign_ref, table_ref, out_ref, rows, place):
    step = pl.program_id(0)
    local_rows, width = raw_ref.shape
    high_count, low_count = table_ref.shape

    @pl.when(step == 0)
    def _():
        rows[:, :width] = normalize_rows(raw_ref[...])
        cluster = assign_ref[...]
        high, low = lax.div(cluster, low_count), lax.rem(cluster, low_count)
        high_hits = lax.broadcasted_iota(jnp.int32, (high_count, local_rows), 0) == high
        by_low = lax.dot_general(
            table_ref[...].astype(jnp.float32).astype(jnp.bfloat16),
            jnp.where(high_hits, 1.0, 0.0).astype(jnp.bfloat16),
            (((0,), (0,)), ((), ())),
            preferred_element_type=jnp.float32,
        )
        low_hits = lax.broadcasted_iota(jnp.int32, (low_count, local_rows), 0) == low
        owner = jnp.sum(jnp.where(low_hits, by_low, 0.0), axis=0, keepdims=True).astype(jnp.int32)
        owner_hits = lax.broadcasted_iota(jnp.int32, (devices, local_rows), 0) == owner
        group = min(128, local_rows)
        earlier = lax.broadcasted_iota(jnp.int32, (group, group), 0) < (
            lax.broadcasted_iota(jnp.int32, (group, group), 1)
        )
        earlier = jnp.where(earlier, 1.0, 0.0).astype(jnp.bfloat16)
        ones = jnp.where(owner_hits, 1.0, 0.0)
        before, seen = [], jnp.zeros((devices, 1), jnp.float32)
        for at in range(0, local_rows, group):
            some = ones[:, at : at + group]
            before.append(
                jnp.dot(some.astype(jnp.bfloat16), earlier, preferred_element_type=jnp.float32) + seen
            )
            seen = seen + jnp.sum(some, axis=1, keepdims=True)
        before = jnp.concatenate(before, axis=1)
        slot = jnp.sum(jnp.where(owner_hits, before, 0.0), axis=0, keepdims=True).astype(jnp.int32)
        owner_dp, owner_depth = lax.div(owner, cent_count), lax.rem(owner, cent_count)
        distance = lax.rem(owner_depth + cent_count - depth_ref[0], cent_count)
        place[...] = (owner_dp * cent_count + distance) * capacity + slot
        number = cluster + 1
        lane = lax.broadcasted_iota(jnp.int32, (LABEL_LANES, local_rows), 0)
        digits = jnp.where(
            lane == 0, lax.div(number, 256), jnp.where(lane == 1, lax.rem(number, 256), 0)
        )
        rows[:, width:] = digits.astype(jnp.float32).T.astype(jnp.bfloat16)

    size = out_ref.shape[0]
    taken = lax.broadcasted_iota(jnp.int32, (size, local_rows), 0) + step * size == place[...]
    taken = jnp.where(taken, 1.0, 0.0).astype(jnp.bfloat16)
    out_ref[...] = jnp.dot(taken, rows[...], preferred_element_type=jnp.float32).astype(jnp.bfloat16)


def pack(embeddings, assign, owner_map, depth, devices, cent_count, capacity):
    local_rows, width = embeddings.shape
    slots = devices * capacity
    tile = min(512, slots)
    low_count = 128
    return call(
        functools.partial(pack_kernel, devices, cent_count, capacity),
        "pack",
        FULL,
        2 * slots * width * local_rows,
        grid=(slots // tile,),
        in_specs=[pl.BlockSpec(memory_space=pltpu.SMEM), whole(), whole(), whole()],
        out_specs=pl.BlockSpec((tile, width + LABEL_LANES), lambda i: (i, 0)),
        out_shape=jax.ShapeDtypeStruct((slots, width + LABEL_LANES), jnp.bfloat16),
        scratch_shapes=[
            pltpu.VMEM((local_rows, width + LABEL_LANES), jnp.bfloat16),
            pltpu.VMEM((1, local_rows), jnp.int32),
        ],
    )(
        depth.reshape(1).astype(jnp.int32),
        embeddings,
        assign.reshape(1, local_rows),
        owner_map.reshape(-1, low_count),
    )


def order_kernel(*refs):
    del refs


def order(value, after):
    return call(
        order_kernel,
        "order",
        FULL,
        1,
        in_specs=[in_hbm()] * (1 + len(after)),
        out_specs=in_hbm(),
        out_shape=jax.ShapeDtypeStruct(value.shape, value.dtype),
        input_output_aliases={0: 0},
    )(value, *after)


def hold_kernel(value_ref, *rest):
    rest[-1][...] = value_ref[...]


def hold(value, after):
    return call(
        hold_kernel,
        "hold",
        8,
        value.size,
        in_specs=[whole()] + [in_hbm()] * len(after),
        out_specs=whole(),
        out_shape=jax.ShapeDtypeStruct(value.shape, value.dtype),
    )(value, *after)


def similarity_kernel(cent_count, first, depth_ref, *rest):
    block_refs = rest[:cent_count]
    out_ref, flag_ref, gathered, column, row, sem = rest[-6:]
    step = pl.program_id(0)
    dp_count, _, capacity, lanes = gathered.shape
    size, slots = out_ref.shape[1:]
    width = lanes - LABEL_LANES

    @pl.when(step == 0)
    def _():
        arriving = []
        for k in range(cent_count):
            source = lax.rem(depth_ref[0] + cent_count - k, cent_count)
            block = block_refs[k].at[:, 0] if k == 0 else block_refs[k]
            arriving.append(pltpu.make_async_copy(block, gathered.at[:, source], sem.at[k]))
            arriving[-1].start()
        for copy in arriving:
            copy.wait()
        digits = gathered[:, :, :, width:].reshape(slots, LABEL_LANES).astype(jnp.float32)
        number = digits[:, 0:1] * 256.0 + digits[:, 1:2]
        column[...] = jnp.where(number > 0.0, number, -1.0)
        across = digits.T
        row[...] = across[0:1] * 256.0 + across[1:2]
        flag_ref[...] = jnp.zeros_like(flag_ref)

    per_step = size // (cent_count * capacity)
    start = pl.multiple_of((first + step) * size, size)
    rows = gathered[pl.ds((first + step) * per_step, per_step), :, :, :width].reshape(size, width)
    every = gathered[:, :, :, :width].reshape(slots, width)
    same = column[pl.ds(start, size)] == row[...]
    out_ref[0] = jnp.where(
        same, contract_final_axis(rows, every) * math.sqrt(width), 0.0
    ).astype(jnp.bfloat16)
    main_diagonal = lax.broadcasted_iota(jnp.int32, (size, size), 0) == (
        lax.broadcasted_iota(jnp.int32, (size, size), 1)
    )
    corner = out_ref[0, :, pl.ds(start, size)]
    out_ref[0, :, pl.ds(start, size)] = jnp.where(
        main_diagonal, 0.0, corner.astype(jnp.float32)
    ).astype(jnp.bfloat16)


def similarity_of(blocks, depth, part, parts, held):
    cent_count = len(blocks)
    dp_count, capacity, lanes = blocks[1].shape
    slots = cent_count * dp_count * capacity
    tile = min(256, slots // parts)
    steps = slots // tile // parts
    aliased = [] if held is None else [held]
    return call(
        functools.partial(similarity_kernel, cent_count, part * steps),
        "similarity",
        FULL,
        2 * slots * slots * lanes // parts,
        grid=(steps,),
        in_specs=[pl.BlockSpec(memory_space=pltpu.SMEM)] + [in_hbm()] * (cent_count + len(aliased)),
        out_specs=[
            pl.BlockSpec((1, tile, slots), lambda i: (0, part * steps + i, 0)),
            pl.BlockSpec((8, 128), lambda i: (0, 0)),
        ],
        out_shape=[
            jax.ShapeDtypeStruct((1, slots, slots), jnp.bfloat16),
            jax.ShapeDtypeStruct((8, 128), jnp.float32),
        ],
        scratch_shapes=[
            pltpu.VMEM((dp_count, cent_count, capacity, lanes), jnp.bfloat16),
            pltpu.VMEM((slots, 1), jnp.float32),
            pltpu.VMEM((1, slots), jnp.float32),
            pltpu.SemaphoreType.DMA((cent_count,)),
        ],
        input_output_aliases={1 + cent_count: 0} if aliased else {},
    )(depth.reshape(1).astype(jnp.int32), *blocks, *aliased)


def shards(embeddings, init_centroids, assign, owner_map):
    devices = lax.axis_size(AXES)
    cent_count = lax.axis_size("cent")
    dp_count = lax.axis_size("dp")
    depth = lax.axis_index("cent")
    local_rows, feature_width = embeddings.shape
    planes = dp_count // 2
    core = lax.axis_index("dp") % 2
    half = init_centroids.shape[0] // 2
    share = half // planes
    capacity = 2 * local_rows // devices
    group_rows = cent_count * local_rows

    def send(value, step):
        return lax.ppermute(
            value, "cent", [(z, (z + step) % cent_count) for z in range(cent_count)]
        )

    def exchange(value):
        return lax.all_to_all(value, "dp", 0, 0, tiled=True)

    same_core = [[2 * chip + c for chip in range(planes)] for c in range(2)]
    other_core = [(i, i + 1 - 2 * (i % 2)) for i in range(dp_count)]

    def exchange_plane(value):
        return lax.all_to_all(value, "dp", 0, 0, axis_index_groups=same_core, tiled=True)

    def swap_cores(value):
        return lax.ppermute(value, "dp", other_core)

    cut = local_rows // 2
    below, above = send(embeddings, 1), send(embeddings, -1)
    far_first, far_second = send(below[:cut], 1), send(above[cut:], -1)
    sources = [embeddings, above, far_first, far_second, below]

    packed = pack(embeddings, assign, owner_map, depth, devices, cent_count, capacity)
    routed = exchange(packed.reshape(dp_count, cent_count * capacity, -1)).reshape(
        dp_count, cent_count, capacity, -1
    )
    initial = normalize_rows(init_centroids)
    own_half = lax.dynamic_slice_in_dim(initial, core * half, half, 0)
    other_half = lax.dynamic_slice_in_dim(initial, (1 - core) * half, half, 0)
    block = jnp.concatenate([own_half, other_half])
    scored = [
        score_piece(raws, block, cut, cost)
        for raws, cost in [
            ([embeddings], OWN_COST),
            ([above], NEAR_COST),
            ([far_first, far_second], FAR_COST),
            ([below], NEAR_COST),
        ]
    ]
    members = [member for *parts, _, _ in scored for member in parts]
    partial_total = jnp.concatenate([total for *_, total, _ in scored], axis=1)
    scale = jnp.concatenate([scale for *_, scale in scored], axis=1)

    totals = [partial_total] + [send(partial_total, -k) for k in range(1, cent_count)]
    parted = [routed[:, k] for k in range(cent_count)]
    sums = weighted_sums(members, sources, scale, totals, core, planes, parted[1:])
    arrived = exchange(sums.reshape(dp_count, share, feature_width))

    blocks = [routed, send(parted[1], 1), None, send(parted[3], -1)]
    blocks[2] = send(order(parted[2], [blocks[1], blocks[3]]), 2)

    own_half = exchange_plane(combine(arrived, planes, [])).reshape(half, feature_width)
    members, partial_total = score_rows(sources, scale, own_half, swap_cores(own_half), cut)
    totals = [partial_total] + [send(partial_total, -k) for k in range(1, cent_count)]
    sums = weighted_sums(members, sources, scale, totals, core, planes, [blocks[2]])
    arrived = exchange(sums.reshape(dp_count, share, feature_width))
    similarity, upper = similarity_of(blocks, depth, 0, 2, None)
    spread = combine(arrived, planes, [upper])
    similarity, lower = similarity_of(blocks, depth, 1, 2, similarity)
    own_half = hold(exchange_plane(spread).reshape(half, feature_width), [lower])
    return (finish(own_half, swap_cores(own_half), core), similarity)


def solution(mesh):
    return jax.shard_map(
        shards,
        mesh=mesh,
        in_specs=(P(AXES, None), P("cent", None), P(AXES), P()),
        out_specs=(P("cent", None), P(AXES, None, None)),
        check_vma=False,
    )
```

```python
import functools
import math

import jax
import jax.numpy as jnp
from jax import lax
from jax.experimental import pallas as pl
from jax.experimental.pallas import tpu as pltpu
from jax.sharding import PartitionSpec as P

ROUNDS = 2
AXES = ("dp", "cent")

epsilon = 1e-06
logit_divisor = 0.02
MIB = 1024 * 1024
LABEL_LANES = 128
NEAR_COST = 1_000_000
OWN_COST = 6_000_000_000
FAR_COST = 50_000_000_000
FULL = 61


def unit(matrix):
    wide = matrix.astype(jnp.float32)
    return wide * (1.0 / jnp.sqrt(jnp.sum(wide * wide, axis=-1, keepdims=True) + epsilon))


def normalize_rows(matrix):
    return unit(matrix).astype(jnp.bfloat16)


def contract_final_axis(left, right):
    return lax.dot_general(
        left, right, (((1,), (1,)), ((), ())), preferred_element_type=jnp.float32
    )


def whole():
    return pl.BlockSpec(memory_space=pltpu.VMEM)


def in_hbm():
    return pl.BlockSpec(memory_space=pl.ANY)


def call(kernel, name, vmem, flops, **options):
    return pl.pallas_call(
        kernel,
        name=name,
        cost_estimate=pl.CostEstimate(flops=int(flops), bytes_accessed=1 << 20, transcendentals=0),
        compiler_params=pltpu.CompilerParams(vmem_limit_bytes=vmem * MIB),
        **options,
    )


def membership_of(block, rows, scale):
    scores = contract_final_axis(block, rows)
    membership = jnp.exp2(scores * (scale * (math.log2(math.e) / logit_divisor)))
    return membership.astype(jnp.bfloat16), jnp.sum(membership, axis=0, keepdims=True)


def piece_kernel(sources, block_ref, *rest):
    raw_refs, member_refs = rest[:sources], rest[sources:-2]
    total_ref, scale_ref = rest[-2:]
    size = member_refs[0].shape[1]
    parts = [(ref, at) for ref in raw_refs for at in range(0, ref.shape[0], size)]
    for i, (ref, start) in enumerate(parts):
        raw = ref[start : start + size]
        at = slice(i * size, (i + 1) * size)
        wide = raw.astype(jnp.float32)
        squares = jnp.sum(wide * wide, axis=-1, keepdims=True) + epsilon
        scale = (1.0 / jnp.sqrt(jnp.broadcast_to(squares, (size, 8)))).T[:1]
        scale_ref[:, at] = scale
        member_refs[i][...], total_ref[:, at] = membership_of(block_ref[...], raw, scale)


def score_piece(raws, block, size, cost):
    rows = sum(raw.shape[0] for raw in raws)
    count = block.shape[0]
    line = jax.ShapeDtypeStruct((1, rows), jnp.float32)
    pieces = rows // size
    return call(
        functools.partial(piece_kernel, len(raws)),
        "score_piece",
        12,
        cost,
        in_specs=[whole()] * (1 + len(raws)),
        out_specs=[whole()] * (pieces + 2),
        out_shape=[jax.ShapeDtypeStruct((count, size), jnp.bfloat16)] * pieces + [line] * 2,
    )(block, *raws)


def fetches(sources, size, taken, sems):
    parts = [
        source.at[pl.ds(at, size)] for source in sources for at in range(0, source.shape[0], size)
    ]
    return [
        pltpu.make_async_copy(part, taken.at[pl.ds(i * size, size)], sems.at[i])
        for i, part in enumerate(parts)
    ]


def score_kernel(pieces, scale_ref, own_ref, other_ref, *rest):
    *sources, total_ref, taken, members, block, in_sem, out_sem = rest
    sources, member_refs = sources[:-pieces], sources[-pieces:]
    half = own_ref.shape[0]
    size = members.shape[2]
    arriving = fetches(sources, size, taken, in_sem)
    for copy in arriving:
        copy.start()
    block[:half], block[half:] = own_ref[...], other_ref[...]
    leaving = []
    for i in range(pieces):
        arriving[i].wait()
        at = slice(i * size, (i + 1) * size)
        members[i], total_ref[:, at] = membership_of(block[...], taken[at], scale_ref[:, at])
        leaving.append(pltpu.make_async_copy(members.at[i], member_refs[i], out_sem.at[i]))
        leaving[-1].start()
    for copy in leaving:
        copy.wait()


def score_rows(sources, scale, own_half, other_half, size):
    pieces = scale.shape[1] // size
    width = sources[0].shape[1]
    count = 2 * own_half.shape[0]
    each = pltpu.SemaphoreType.DMA((pieces,))
    out = call(
        functools.partial(score_kernel, pieces),
        "score_rows",
        FULL,
        NEAR_COST,
        in_specs=[whole()] * 3 + [in_hbm()] * len(sources),
        out_specs=[in_hbm()] * pieces + [whole()],
        out_shape=[jax.ShapeDtypeStruct((count, size), jnp.bfloat16)] * pieces
        + [jax.ShapeDtypeStruct((1, pieces * size), jnp.float32)],
        scratch_shapes=[
            pltpu.VMEM((pieces * size, width), jnp.bfloat16),
            pltpu.VMEM((pieces, count, size), jnp.bfloat16),
            pltpu.VMEM((count, width), jnp.bfloat16),
            each,
            each,
        ],
    )(scale, own_half, other_half, *sources)
    return out[:pieces], out[pieces]


def sum_kernel(pieces, depth, source_count, outs, core_ref, scale_ref, *rest):
    total_refs, rest = rest[:depth], rest[depth:]
    *rest, members, taken, running, member_sem, row_sem = rest
    out_refs = rest[-outs:]
    member_refs, sources = rest[:pieces], rest[pieces : pieces + source_count]
    half = running.shape[0] // 2
    size = members.shape[2]
    arriving = [
        (rows, pltpu.make_async_copy(member_refs[i], members.at[i], member_sem.at[i]))
        for i, rows in enumerate(fetches(sources, size, taken, row_sem))
    ]
    for pair in arriving:
        for copy in pair:
            copy.start()
    for i in range(pieces):
        for copy in arriving[i]:
            copy.wait()
        at = slice(i * size, (i + 1) * size)
        total = total_refs[0][:, at]
        for k in range(1, depth):
            j = (i + pieces - k * (pieces // depth)) % pieces
            total = total + total_refs[k][:, j * size : (j + 1) * size]
        weights = members[i].astype(jnp.float32) * (scale_ref[:, at] / total)
        product = jnp.dot(
            weights.astype(jnp.bfloat16), taken[at], preferred_element_type=jnp.float32
        )
        if i == 0:
            running[...] = product
        else:
            running[...] += product
    own, other = running[:half].astype(jnp.bfloat16), running[half:].astype(jnp.bfloat16)
    if outs == 2:
        out_refs[0][...], out_refs[1][...] = own, other
    else:
        chips, _, share, width = out_refs[0].shape
        out_refs[0][:, core_ref[0]] = own.reshape(chips, share, width)
        out_refs[0][:, 1 - core_ref[0]] = other.reshape(chips, share, width)


def weighted_sums(members, sources, scale, totals, core, chips, after):
    pieces = len(members)
    count, size = members[0].shape
    width = sources[0].shape[1]
    half = count // 2
    shapes = [(chips, 2, half // chips, width)] if chips else [(half, width)] * 2
    return call(
        functools.partial(sum_kernel, pieces, len(totals), len(sources), len(shapes)),
        "weighted_sums",
        FULL,
        2 * pieces * size * width * count,
        in_specs=[pl.BlockSpec(memory_space=pltpu.SMEM)]
        + [whole()] * (1 + len(totals))
        + [in_hbm()] * (pieces + len(sources))
        + [in_hbm()] * len(after),
        out_specs=[whole()] * len(shapes),
        out_shape=[jax.ShapeDtypeStruct(shape, jnp.bfloat16) for shape in shapes],
        scratch_shapes=[
            pltpu.VMEM((pieces, count, size), jnp.bfloat16),
            pltpu.VMEM((pieces * size, width), jnp.bfloat16),
            pltpu.VMEM((count, width), jnp.float32),
            pltpu.SemaphoreType.DMA((pieces,)),
            pltpu.SemaphoreType.DMA((pieces,)),
        ],
    )(core.reshape(1).astype(jnp.int32), scale, *totals, *members, *sources, *after)


def combine_kernel(arrived_ref, *rest):
    spread_ref = rest[-1]
    total = arrived_ref[0].astype(jnp.float32)
    for i in range(1, arrived_ref.shape[0]):
        total = total + arrived_ref[i].astype(jnp.float32)
    share = normalize_rows(total)
    for i in range(spread_ref.shape[0]):
        spread_ref[i] = share


def combine(arrived, receivers, after):
    return call(
        combine_kernel,
        "combine",
        8,
        2 * arrived.size,
        in_specs=[whole()] + [in_hbm()] * len(after),
        out_specs=whole(),
        out_shape=jax.ShapeDtypeStruct((receivers,) + arrived.shape[1:], arrived.dtype),
    )(arrived, *after)


def finish_kernel(core_ref, own_ref, other_ref, out_ref):
    half, width = own_ref.shape
    core = core_ref[0]
    for side, ref in ((core, own_ref), (1 - core, other_ref)):
        at = pl.ds(pl.multiple_of(side * half, half), half)
        out_ref[at] = ref[...].astype(jnp.float32) * math.sqrt(width)


def finish(own_half, other_half, core):
    half, width = own_half.shape
    return call(
        finish_kernel,
        "finish",
        8,
        own_half.size,
        in_specs=[pl.BlockSpec(memory_space=pltpu.SMEM), whole(), whole()],
        out_specs=whole(),
        out_shape=jax.ShapeDtypeStruct((2 * half, width), jnp.float32),
    )(core.reshape(1).astype(jnp.int32), own_half, other_half)


def pack_kernel(devices, cent_count, capacity, depth_ref, raw_ref, assign_ref, table_ref, out_ref, rows, place):
    step = pl.program_id(0)
    local_rows, width = raw_ref.shape
    high_count, low_count = table_ref.shape

    @pl.when(step == 0)
    def _():
        rows[:, :width] = normalize_rows(raw_ref[...])
        cluster = assign_ref[...]
        high, low = lax.div(cluster, low_count), lax.rem(cluster, low_count)
        high_hits = lax.broadcasted_iota(jnp.int32, (high_count, local_rows), 0) == high
        by_low = lax.dot_general(
            table_ref[...].astype(jnp.float32).astype(jnp.bfloat16),
            jnp.where(high_hits, 1.0, 0.0).astype(jnp.bfloat16),
            (((0,), (0,)), ((), ())),
            preferred_element_type=jnp.float32,
        )
        low_hits = lax.broadcasted_iota(jnp.int32, (low_count, local_rows), 0) == low
        owner = jnp.sum(jnp.where(low_hits, by_low, 0.0), axis=0, keepdims=True).astype(jnp.int32)
        owner_hits = lax.broadcasted_iota(jnp.int32, (devices, local_rows), 0) == owner
        group = min(128, local_rows)
        earlier = lax.broadcasted_iota(jnp.int32, (group, group), 0) < (
            lax.broadcasted_iota(jnp.int32, (group, group), 1)
        )
        earlier = jnp.where(earlier, 1.0, 0.0).astype(jnp.bfloat16)
        ones = jnp.where(owner_hits, 1.0, 0.0)
        before, seen = [], jnp.zeros((devices, 1), jnp.float32)
        for at in range(0, local_rows, group):
            some = ones[:, at : at + group]
            before.append(
                jnp.dot(some.astype(jnp.bfloat16), earlier, preferred_element_type=jnp.float32) + seen
            )
            seen = seen + jnp.sum(some, axis=1, keepdims=True)
        before = jnp.concatenate(before, axis=1)
        slot = jnp.sum(jnp.where(owner_hits, before, 0.0), axis=0, keepdims=True).astype(jnp.int32)
        owner_dp, owner_depth = lax.div(owner, cent_count), lax.rem(owner, cent_count)
        distance = lax.rem(owner_depth + cent_count - depth_ref[0], cent_count)
        place[...] = (owner_dp * cent_count + distance) * capacity + slot
        number = cluster + 1
        lane = lax.broadcasted_iota(jnp.int32, (LABEL_LANES, local_rows), 0)
        digits = jnp.where(
            lane == 0, lax.div(number, 256), jnp.where(lane == 1, lax.rem(number, 256), 0)
        )
        rows[:, width:] = digits.astype(jnp.float32).T.astype(jnp.bfloat16)

    size = out_ref.shape[0]
    taken = lax.broadcasted_iota(jnp.int32, (size, local_rows), 0) + step * size == place[...]
    taken = jnp.where(taken, 1.0, 0.0).astype(jnp.bfloat16)
    out_ref[...] = jnp.dot(taken, rows[...], preferred_element_type=jnp.float32).astype(jnp.bfloat16)


def pack(embeddings, assign, owner_map, depth, devices, cent_count, capacity):
    local_rows, width = embeddings.shape
    slots = devices * capacity
    tile = min(512, slots)
    low_count = 128
    return call(
        functools.partial(pack_kernel, devices, cent_count, capacity),
        "pack",
        FULL,
        2 * slots * width * local_rows,
        grid=(slots // tile,),
        in_specs=[pl.BlockSpec(memory_space=pltpu.SMEM), whole(), whole(), whole()],
        out_specs=pl.BlockSpec((tile, width + LABEL_LANES), lambda i: (i, 0)),
        out_shape=jax.ShapeDtypeStruct((slots, width + LABEL_LANES), jnp.bfloat16),
        scratch_shapes=[
            pltpu.VMEM((local_rows, width + LABEL_LANES), jnp.bfloat16),
            pltpu.VMEM((1, local_rows), jnp.int32),
        ],
    )(
        depth.reshape(1).astype(jnp.int32),
        embeddings,
        assign.reshape(1, local_rows),
        owner_map.reshape(-1, low_count),
    )


def order_kernel(*refs):
    del refs


def order(value, after):
    return call(
        order_kernel,
        "order",
        FULL,
        1,
        in_specs=[in_hbm()] * (1 + len(after)),
        out_specs=in_hbm(),
        out_shape=jax.ShapeDtypeStruct(value.shape, value.dtype),
        input_output_aliases={0: 0},
    )(value, *after)


def hold_kernel(value_ref, *rest):
    rest[-1][...] = value_ref[...]


def hold(value, after):
    return call(
        hold_kernel,
        "hold",
        8,
        value.size,
        in_specs=[whole()] + [in_hbm()] * len(after),
        out_specs=whole(),
        out_shape=jax.ShapeDtypeStruct(value.shape, value.dtype),
    )(value, *after)


def similarity_kernel(cent_count, first, depth_ref, *rest):
    block_refs = rest[:cent_count]
    out_ref, flag_ref, gathered, column, row, sem = rest[-6:]
    step = pl.program_id(0)
    dp_count, _, capacity, lanes = gathered.shape
    size, slots = out_ref.shape[1:]
    width = lanes - LABEL_LANES

    @pl.when(step == 0)
    def _():
        arriving = []
        for k in range(cent_count):
            source = lax.rem(depth_ref[0] + cent_count - k, cent_count)
            block = block_refs[k].at[:, 0] if k == 0 else block_refs[k]
            arriving.append(pltpu.make_async_copy(block, gathered.at[:, source], sem.at[k]))
            arriving[-1].start()
        for copy in arriving:
            copy.wait()
        digits = gathered[:, :, :, width:].reshape(slots, LABEL_LANES).astype(jnp.float32)
        number = digits[:, 0:1] * 256.0 + digits[:, 1:2]
        column[...] = jnp.where(number > 0.0, number, -1.0)
        across = digits.T
        row[...] = across[0:1] * 256.0 + across[1:2]
        flag_ref[...] = jnp.zeros_like(flag_ref)

    per_step = size // (cent_count * capacity)
    start = pl.multiple_of((first + step) * size, size)
    rows = gathered[pl.ds((first + step) * per_step, per_step), :, :, :width].reshape(size, width)
    every = gathered[:, :, :, :width].reshape(slots, width)
    same = column[pl.ds(start, size)] == row[...]
    out_ref[0] = jnp.where(
        same, contract_final_axis(rows, every) * math.sqrt(width), 0.0
    ).astype(jnp.bfloat16)
    main_diagonal = lax.broadcasted_iota(jnp.int32, (size, size), 0) == (
        lax.broadcasted_iota(jnp.int32, (size, size), 1)
    )
    corner = out_ref[0, :, pl.ds(start, size)]
    out_ref[0, :, pl.ds(start, size)] = jnp.where(
        main_diagonal, 0.0, corner.astype(jnp.float32)
    ).astype(jnp.bfloat16)


def similarity_of(blocks, depth, part, parts, held):
    cent_count = len(blocks)
    dp_count, capacity, lanes = blocks[1].shape
    slots = cent_count * dp_count * capacity
    tile = min(256, slots // parts)
    steps = slots // tile // parts
    aliased = [] if held is None else [held]
    return call(
        functools.partial(similarity_kernel, cent_count, part * steps),
        "similarity",
        FULL,
        2 * slots * slots * lanes // parts,
        grid=(steps,),
        in_specs=[pl.BlockSpec(memory_space=pltpu.SMEM)] + [in_hbm()] * (cent_count + len(aliased)),
        out_specs=[
            pl.BlockSpec((1, tile, slots), lambda i: (0, part * steps + i, 0)),
            pl.BlockSpec((8, 128), lambda i: (0, 0)),
        ],
        out_shape=[
            jax.ShapeDtypeStruct((1, slots, slots), jnp.bfloat16),
            jax.ShapeDtypeStruct((8, 128), jnp.float32),
        ],
        scratch_shapes=[
            pltpu.VMEM((dp_count, cent_count, capacity, lanes), jnp.bfloat16),
            pltpu.VMEM((slots, 1), jnp.float32),
            pltpu.VMEM((1, slots), jnp.float32),
            pltpu.SemaphoreType.DMA((cent_count,)),
        ],
        input_output_aliases={1 + cent_count: 0} if aliased else {},
    )(depth.reshape(1).astype(jnp.int32), *blocks, *aliased)


def shards(embeddings, init_centroids, assign, owner_map):
    devices = lax.axis_size(AXES)
    cent_count = lax.axis_size("cent")
    dp_count = lax.axis_size("dp")
    depth = lax.axis_index("cent")
    local_rows, feature_width = embeddings.shape
    planes = dp_count // 2
    core = lax.axis_index("dp") % 2
    half = init_centroids.shape[0] // 2
    share = half // planes
    capacity = 2 * local_rows // devices
    group_rows = cent_count * local_rows

    def send(value, step):
        return lax.ppermute(
            value, "cent", [(z, (z + step) % cent_count) for z in range(cent_count)]
        )

    def exchange(value):
        return lax.all_to_all(value, "dp", 0, 0, tiled=True)

    same_core = [[2 * chip + c for chip in range(planes)] for c in range(2)]
    other_core = [(i, i + 1 - 2 * (i % 2)) for i in range(dp_count)]

    def exchange_plane(value):
        return lax.all_to_all(value, "dp", 0, 0, axis_index_groups=same_core, tiled=True)

    def swap_cores(value):
        return lax.ppermute(value, "dp", other_core)

    cut = local_rows // 2
    below, above = send(embeddings, 1), send(embeddings, -1)
    far_first, far_second = send(below[:cut], 1), send(above[cut:], -1)
    sources = [embeddings, above, far_first, far_second, below]

    packed = pack(embeddings, assign, owner_map, depth, devices, cent_count, capacity)
    routed = exchange(packed.reshape(dp_count, cent_count * capacity, -1)).reshape(
        dp_count, cent_count, capacity, -1
    )
    initial = normalize_rows(init_centroids)
    own_half = lax.dynamic_slice_in_dim(initial, core * half, half, 0)
    other_half = lax.dynamic_slice_in_dim(initial, (1 - core) * half, half, 0)
    block = jnp.concatenate([own_half, other_half])
    scored = [
        score_piece(raws, block, cut, cost)
        for raws, cost in [
            ([embeddings], OWN_COST),
            ([above], NEAR_COST),
            ([far_first, far_second], FAR_COST),
            ([below], NEAR_COST),
        ]
    ]
    members = [member for *parts, _, _ in scored for member in parts]
    partial_total = jnp.concatenate([total for *_, total, _ in scored], axis=1)
    scale = jnp.concatenate([scale for *_, scale in scored], axis=1)

    totals = [partial_total] + [send(partial_total, -k) for k in range(1, cent_count)]
    parted = [routed[:, k] for k in range(cent_count)]
    own, for_sibling = weighted_sums(members, sources, scale, totals, core, 0, parted[1:])
    both = (own.astype(jnp.float32) + swap_cores(for_sibling).astype(jnp.float32)).astype(jnp.bfloat16)
    arrived = exchange_plane(both.reshape(planes, share, feature_width))

    blocks = [routed, send(parted[1], 1), None, send(parted[3], -1)]
    blocks[2] = send(order(parted[2], [blocks[1], blocks[3]]), 2)

    own_half = exchange_plane(combine(arrived, planes, [])).reshape(half, feature_width)
    members, partial_total = score_rows(sources, scale, own_half, swap_cores(own_half), cut)
    totals = [partial_total] + [send(partial_total, -k) for k in range(1, cent_count)]
    (sums,) = weighted_sums(members, sources, scale, totals, core, planes, [blocks[2]])
    arrived = exchange(sums.reshape(dp_count, share, feature_width))
    similarity, upper = similarity_of(blocks, depth, 0, 2, None)
    spread = combine(arrived, planes, [upper])
    similarity, lower = similarity_of(blocks, depth, 1, 2, similarity)
    own_half = hold(exchange_plane(spread).reshape(half, feature_width), [lower])
    return (finish(own_half, swap_cores(own_half), core), similarity)


def solution(mesh):
    return jax.shard_map(
        shards,
        mesh=mesh,
        in_specs=(P(AXES, None), P("cent", None), P(AXES), P()),
        out_specs=(P("cent", None), P(AXES, None, None)),
        check_vma=False,
    )
```

```python
import functools
import math

import jax
import jax.numpy as jnp
from jax import lax
from jax.experimental import pallas as pl
from jax.experimental.pallas import tpu as pltpu
from jax.sharding import PartitionSpec as P

ROUNDS = 2
AXES = ("dp", "cent")

epsilon = 1e-06
logit_divisor = 0.02
MIB = 1024 * 1024
LABEL_LANES = 128
NEAR_COST = 1_000_000
OWN_COST = 6_000_000_000
FAR_COST = 50_000_000_000
FULL = 61


def unit(matrix):
    wide = matrix.astype(jnp.float32)
    return wide * (1.0 / jnp.sqrt(jnp.sum(wide * wide, axis=-1, keepdims=True) + epsilon))


def normalize_rows(matrix):
    return unit(matrix).astype(jnp.bfloat16)


def contract_final_axis(left, right):
    return lax.dot_general(
        left, right, (((1,), (1,)), ((), ())), preferred_element_type=jnp.float32
    )


def whole():
    return pl.BlockSpec(memory_space=pltpu.VMEM)


def in_hbm():
    return pl.BlockSpec(memory_space=pl.ANY)


def call(kernel, name, vmem, flops, **options):
    return pl.pallas_call(
        kernel,
        name=name,
        cost_estimate=pl.CostEstimate(flops=int(flops), bytes_accessed=1 << 20, transcendentals=0),
        compiler_params=pltpu.CompilerParams(vmem_limit_bytes=vmem * MIB),
        **options,
    )


def membership_of(block, rows, scale):
    scores = contract_final_axis(block, rows)
    membership = jnp.exp2(scores * (scale * (math.log2(math.e) / logit_divisor)))
    return membership.astype(jnp.bfloat16), jnp.sum(membership, axis=0, keepdims=True)


def piece_kernel(sources, size, block_ref, *rest):
    raw_refs, member_refs = rest[:sources], rest[sources:-2]
    total_ref, scale_ref = rest[-2:]
    parts = [(ref, at) for ref in raw_refs for at in range(0, ref.shape[0], size)]
    for i, (ref, start) in enumerate(parts):
        raw = ref[start : start + size]
        at = slice(i * size, (i + 1) * size)
        wide = raw.astype(jnp.float32)
        squares = jnp.sum(wide * wide, axis=-1, keepdims=True) + epsilon
        scale = (1.0 / jnp.sqrt(jnp.broadcast_to(squares, (size, 8)))).T[:1]
        scale_ref[:, at] = scale
        member, total_ref[:, at] = membership_of(block_ref[...], raw, scale)
        if member_refs:
            member_refs[i][...] = member


def score_piece(raws, block, size, cost, keep):
    rows = sum(raw.shape[0] for raw in raws)
    count = block.shape[0]
    line = jax.ShapeDtypeStruct((1, rows), jnp.float32)
    pieces = rows // size if keep else 0
    return call(
        functools.partial(piece_kernel, len(raws), size),
        "score_piece",
        12,
        cost,
        in_specs=[whole()] * (1 + len(raws)),
        out_specs=[whole()] * (pieces + 2),
        out_shape=[jax.ShapeDtypeStruct((count, size), jnp.bfloat16)] * pieces + [line] * 2,
    )(block, *raws)


def fetches(sources, size, taken, sems):
    parts = [
        source.at[pl.ds(at, size)] for source in sources for at in range(0, source.shape[0], size)
    ]
    return [
        pltpu.make_async_copy(part, taken.at[pl.ds(i * size, size)], sems.at[i])
        for i, part in enumerate(parts)
    ]


def score_kernel(pieces, scale_ref, own_ref, other_ref, *rest):
    *sources, total_ref, taken, members, block, in_sem, out_sem = rest
    sources, member_refs = sources[:-pieces], sources[-pieces:]
    half = own_ref.shape[0]
    size = members.shape[2]
    arriving = fetches(sources, size, taken, in_sem)
    for copy in arriving:
        copy.start()
    block[:half], block[half:] = own_ref[...], other_ref[...]
    leaving = []
    for i in range(pieces):
        arriving[i].wait()
        at = slice(i * size, (i + 1) * size)
        members[i], total_ref[:, at] = membership_of(block[...], taken[at], scale_ref[:, at])
        leaving.append(pltpu.make_async_copy(members.at[i], member_refs[i], out_sem.at[i]))
        leaving[-1].start()
    for copy in leaving:
        copy.wait()


def score_rows(sources, scale, own_half, other_half, size):
    pieces = scale.shape[1] // size
    width = sources[0].shape[1]
    count = 2 * own_half.shape[0]
    each = pltpu.SemaphoreType.DMA((pieces,))
    out = call(
        functools.partial(score_kernel, pieces),
        "score_rows",
        FULL,
        NEAR_COST,
        in_specs=[whole()] * 3 + [in_hbm()] * len(sources),
        out_specs=[in_hbm()] * pieces + [whole()],
        out_shape=[jax.ShapeDtypeStruct((count, size), jnp.bfloat16)] * pieces
        + [jax.ShapeDtypeStruct((1, pieces * size), jnp.float32)],
        scratch_shapes=[
            pltpu.VMEM((pieces * size, width), jnp.bfloat16),
            pltpu.VMEM((pieces, count, size), jnp.bfloat16),
            pltpu.VMEM((count, width), jnp.bfloat16),
            each,
            each,
        ],
    )(scale, own_half, other_half, *sources)
    return out[:pieces], out[pieces]


def sum_kernel(held, depth, source_count, outs, core_ref, scale_ref, block_ref, *rest):
    pieces = len(held)
    total_refs, rest = rest[:depth], rest[depth:]
    *rest, members, taken, running, member_sem, row_sem = rest
    out_refs = rest[-outs:]
    member_refs, sources = iter(rest[: sum(held)]), rest[sum(held) : sum(held) + source_count]
    half = running.shape[0] // 2
    size = members.shape[2]
    arriving = [
        (rows, pltpu.make_async_copy(next(member_refs), members.at[i], member_sem.at[i]))
        if held[i]
        else (rows,)
        for i, rows in enumerate(fetches(sources, size, taken, row_sem))
    ]
    for pair in arriving:
        for copy in pair:
            copy.start()
    for i in range(pieces):
        for copy in arriving[i]:
            copy.wait()
        at = slice(i * size, (i + 1) * size)
        total = total_refs[0][:, at]
        for k in range(1, depth):
            j = (i + pieces - k * (pieces // depth)) % pieces
            total = total + total_refs[k][:, j * size : (j + 1) * size]
        if held[i]:
            member = members[i]
        else:
            member, _ = membership_of(block_ref[...], taken[at], scale_ref[:, at])
        weights = member.astype(jnp.float32) * (scale_ref[:, at] / total)
        product = jnp.dot(
            weights.astype(jnp.bfloat16), taken[at], preferred_element_type=jnp.float32
        )
        if i == 0:
            running[...] = product
        else:
            running[...] += product
    own, other = running[:half].astype(jnp.bfloat16), running[half:].astype(jnp.bfloat16)
    if outs == 2:
        out_refs[0][...], out_refs[1][...] = own, other
    else:
        chips, _, share, width = out_refs[0].shape
        out_refs[0][:, core_ref[0]] = own.reshape(chips, share, width)
        out_refs[0][:, 1 - core_ref[0]] = other.reshape(chips, share, width)


def weighted_sums(members, sources, scale, totals, block, core, chips, after):
    pieces = len(members)
    count, size = members[0].shape
    width = sources[0].shape[1]
    held = tuple(member is not None for member in members)
    half = count // 2
    shapes = [(chips, 2, half // chips, width)] if chips else [(half, width)] * 2
    return call(
        functools.partial(sum_kernel, held, len(totals), len(sources), len(shapes)),
        "weighted_sums",
        FULL,
        2 * pieces * size * width * count,
        in_specs=[pl.BlockSpec(memory_space=pltpu.SMEM)]
        + [whole()] * (2 + len(totals))
        + [in_hbm()] * (sum(held) + len(sources))
        + [in_hbm()] * len(after),
        out_specs=[whole()] * len(shapes),
        out_shape=[jax.ShapeDtypeStruct(shape, jnp.bfloat16) for shape in shapes],
        scratch_shapes=[
            pltpu.VMEM((pieces, count, size), jnp.bfloat16),
            pltpu.VMEM((pieces * size, width), jnp.bfloat16),
            pltpu.VMEM((count, width), jnp.float32),
            pltpu.SemaphoreType.DMA((pieces,)),
            pltpu.SemaphoreType.DMA((pieces,)),
        ],
    )(
        core.reshape(1).astype(jnp.int32),
        scale,
        block,
        *totals,
        *[member for member in members if member is not None],
        *sources,
        *after,
    )


def combine_kernel(arrived_ref, *rest):
    spread_ref = rest[-1]
    total = arrived_ref[0].astype(jnp.float32)
    for i in range(1, arrived_ref.shape[0]):
        total = total + arrived_ref[i].astype(jnp.float32)
    share = normalize_rows(total)
    for i in range(spread_ref.shape[0]):
        spread_ref[i] = share


def combine(arrived, receivers, after):
    return call(
        combine_kernel,
        "combine",
        8,
        2 * arrived.size,
        in_specs=[whole()] + [in_hbm()] * len(after),
        out_specs=whole(),
        out_shape=jax.ShapeDtypeStruct((receivers,) + arrived.shape[1:], arrived.dtype),
    )(arrived, *after)


def finish_kernel(core_ref, own_ref, other_ref, out_ref):
    half, width = own_ref.shape
    core = core_ref[0]
    for side, ref in ((core, own_ref), (1 - core, other_ref)):
        at = pl.ds(pl.multiple_of(side * half, half), half)
        out_ref[at] = ref[...].astype(jnp.float32) * math.sqrt(width)


def finish(own_half, other_half, core):
    half, width = own_half.shape
    return call(
        finish_kernel,
        "finish",
        8,
        own_half.size,
        in_specs=[pl.BlockSpec(memory_space=pltpu.SMEM), whole(), whole()],
        out_specs=whole(),
        out_shape=jax.ShapeDtypeStruct((2 * half, width), jnp.float32),
    )(core.reshape(1).astype(jnp.int32), own_half, other_half)


def pack_kernel(devices, cent_count, capacity, depth_ref, raw_ref, assign_ref, table_ref, out_ref, rows, place):
    step = pl.program_id(0)
    local_rows, width = raw_ref.shape
    high_count, low_count = table_ref.shape

    @pl.when(step == 0)
    def _():
        rows[:, :width] = normalize_rows(raw_ref[...])
        cluster = assign_ref[...]
        high, low = lax.div(cluster, low_count), lax.rem(cluster, low_count)
        high_hits = lax.broadcasted_iota(jnp.int32, (high_count, local_rows), 0) == high
        by_low = lax.dot_general(
            table_ref[...].astype(jnp.float32).astype(jnp.bfloat16),
            jnp.where(high_hits, 1.0, 0.0).astype(jnp.bfloat16),
            (((0,), (0,)), ((), ())),
            preferred_element_type=jnp.float32,
        )
        low_hits = lax.broadcasted_iota(jnp.int32, (low_count, local_rows), 0) == low
        owner = jnp.sum(jnp.where(low_hits, by_low, 0.0), axis=0, keepdims=True).astype(jnp.int32)
        owner_hits = lax.broadcasted_iota(jnp.int32, (devices, local_rows), 0) == owner
        group = min(128, local_rows)
        earlier = lax.broadcasted_iota(jnp.int32, (group, group), 0) < (
            lax.broadcasted_iota(jnp.int32, (group, group), 1)
        )
        earlier = jnp.where(earlier, 1.0, 0.0).astype(jnp.bfloat16)
        ones = jnp.where(owner_hits, 1.0, 0.0)
        before, seen = [], jnp.zeros((devices, 1), jnp.float32)
        for at in range(0, local_rows, group):
            some = ones[:, at : at + group]
            before.append(
                jnp.dot(some.astype(jnp.bfloat16), earlier, preferred_element_type=jnp.float32) + seen
            )
            seen = seen + jnp.sum(some, axis=1, keepdims=True)
        before = jnp.concatenate(before, axis=1)
        slot = jnp.sum(jnp.where(owner_hits, before, 0.0), axis=0, keepdims=True).astype(jnp.int32)
        owner_dp, owner_depth = lax.div(owner, cent_count), lax.rem(owner, cent_count)
        distance = lax.rem(owner_depth + cent_count - depth_ref[0], cent_count)
        place[...] = (owner_dp * cent_count + distance) * capacity + slot
        number = cluster + 1
        lane = lax.broadcasted_iota(jnp.int32, (LABEL_LANES, local_rows), 0)
        digits = jnp.where(
            lane == 0, lax.div(number, 256), jnp.where(lane == 1, lax.rem(number, 256), 0)
        )
        rows[:, width:] = digits.astype(jnp.float32).T.astype(jnp.bfloat16)

    size = out_ref.shape[0]
    taken = lax.broadcasted_iota(jnp.int32, (size, local_rows), 0) + step * size == place[...]
    taken = jnp.where(taken, 1.0, 0.0).astype(jnp.bfloat16)
    out_ref[...] = jnp.dot(taken, rows[...], preferred_element_type=jnp.float32).astype(jnp.bfloat16)


def pack(embeddings, assign, owner_map, depth, devices, cent_count, capacity):
    local_rows, width = embeddings.shape
    slots = devices * capacity
    tile = min(512, slots)
    low_count = 128
    return call(
        functools.partial(pack_kernel, devices, cent_count, capacity),
        "pack",
        FULL,
        2 * slots * width * local_rows,
        grid=(slots // tile,),
        in_specs=[pl.BlockSpec(memory_space=pltpu.SMEM), whole(), whole(), whole()],
        out_specs=pl.BlockSpec((tile, width + LABEL_LANES), lambda i: (i, 0)),
        out_shape=jax.ShapeDtypeStruct((slots, width + LABEL_LANES), jnp.bfloat16),
        scratch_shapes=[
            pltpu.VMEM((local_rows, width + LABEL_LANES), jnp.bfloat16),
            pltpu.VMEM((1, local_rows), jnp.int32),
        ],
    )(
        depth.reshape(1).astype(jnp.int32),
        embeddings,
        assign.reshape(1, local_rows),
        owner_map.reshape(-1, low_count),
    )


def order_kernel(*refs):
    del refs


def order(value, after):
    return call(
        order_kernel,
        "order",
        FULL,
        1,
        in_specs=[in_hbm()] * (1 + len(after)),
        out_specs=in_hbm(),
        out_shape=jax.ShapeDtypeStruct(value.shape, value.dtype),
        input_output_aliases={0: 0},
    )(value, *after)


def hold_kernel(value_ref, *rest):
    rest[-1][...] = value_ref[...]


def hold(value, after):
    return call(
        hold_kernel,
        "hold",
        8,
        value.size,
        in_specs=[whole()] + [in_hbm()] * len(after),
        out_specs=whole(),
        out_shape=jax.ShapeDtypeStruct(value.shape, value.dtype),
    )(value, *after)


def similarity_kernel(cent_count, first, depth_ref, *rest):
    block_refs = rest[:cent_count]
    out_ref, flag_ref, gathered, column, row, sem = rest[-6:]
    step = pl.program_id(0)
    dp_count, _, capacity, lanes = gathered.shape
    size, slots = out_ref.shape[1:]
    width = lanes - LABEL_LANES

    @pl.when(step == 0)
    def _():
        arriving = []
        for k in range(cent_count):
            source = lax.rem(depth_ref[0] + cent_count - k, cent_count)
            block = block_refs[k].at[:, 0] if k == 0 else block_refs[k]
            arriving.append(pltpu.make_async_copy(block, gathered.at[:, source], sem.at[k]))
            arriving[-1].start()
        for copy in arriving:
            copy.wait()
        digits = gathered[:, :, :, width:].reshape(slots, LABEL_LANES).astype(jnp.float32)
        number = digits[:, 0:1] * 256.0 + digits[:, 1:2]
        column[...] = jnp.where(number > 0.0, number, -1.0)
        across = digits.T
        row[...] = across[0:1] * 256.0 + across[1:2]
        flag_ref[...] = jnp.zeros_like(flag_ref)

    per_step = size // (cent_count * capacity)
    start = pl.multiple_of((first + step) * size, size)
    rows = gathered[pl.ds((first + step) * per_step, per_step), :, :, :width].reshape(size, width)
    every = gathered[:, :, :, :width].reshape(slots, width)
    same = column[pl.ds(start, size)] == row[...]
    out_ref[0] = jnp.where(
        same, contract_final_axis(rows, every) * math.sqrt(width), 0.0
    ).astype(jnp.bfloat16)
    main_diagonal = lax.broadcasted_iota(jnp.int32, (size, size), 0) == (
        lax.broadcasted_iota(jnp.int32, (size, size), 1)
    )
    corner = out_ref[0, :, pl.ds(start, size)]
    out_ref[0, :, pl.ds(start, size)] = jnp.where(
        main_diagonal, 0.0, corner.astype(jnp.float32)
    ).astype(jnp.bfloat16)


def similarity_of(blocks, depth, part, parts, held):
    cent_count = len(blocks)
    dp_count, capacity, lanes = blocks[1].shape
    slots = cent_count * dp_count * capacity
    tile = min(256, slots // parts)
    steps = slots // tile // parts
    aliased = [] if held is None else [held]
    return call(
        functools.partial(similarity_kernel, cent_count, part * steps),
        "similarity",
        FULL,
        2 * slots * slots * lanes // parts,
        grid=(steps,),
        in_specs=[pl.BlockSpec(memory_space=pltpu.SMEM)] + [in_hbm()] * (cent_count + len(aliased)),
        out_specs=[
            pl.BlockSpec((1, tile, slots), lambda i: (0, part * steps + i, 0)),
            pl.BlockSpec((8, 128), lambda i: (0, 0)),
        ],
        out_shape=[
            jax.ShapeDtypeStruct((1, slots, slots), jnp.bfloat16),
            jax.ShapeDtypeStruct((8, 128), jnp.float32),
        ],
        scratch_shapes=[
            pltpu.VMEM((dp_count, cent_count, capacity, lanes), jnp.bfloat16),
            pltpu.VMEM((slots, 1), jnp.float32),
            pltpu.VMEM((1, slots), jnp.float32),
            pltpu.SemaphoreType.DMA((cent_count,)),
        ],
        input_output_aliases={1 + cent_count: 0} if aliased else {},
    )(depth.reshape(1).astype(jnp.int32), *blocks, *aliased)


def shards(embeddings, init_centroids, assign, owner_map):
    devices = lax.axis_size(AXES)
    cent_count = lax.axis_size("cent")
    dp_count = lax.axis_size("dp")
    depth = lax.axis_index("cent")
    local_rows, feature_width = embeddings.shape
    planes = dp_count // 2
    core = lax.axis_index("dp") % 2
    half = init_centroids.shape[0] // 2
    share = half // planes
    capacity = 2 * local_rows // devices
    group_rows = cent_count * local_rows

    def send(value, step):
        return lax.ppermute(
            value, "cent", [(z, (z + step) % cent_count) for z in range(cent_count)]
        )

    def exchange(value):
        return lax.all_to_all(value, "dp", 0, 0, tiled=True)

    same_core = [[2 * chip + c for chip in range(planes)] for c in range(2)]
    other_core = [(i, i + 1 - 2 * (i % 2)) for i in range(dp_count)]

    def exchange_plane(value):
        return lax.all_to_all(value, "dp", 0, 0, axis_index_groups=same_core, tiled=True)

    def swap_cores(value):
        return lax.ppermute(value, "dp", other_core)

    cut = local_rows // 2
    below, above = send(embeddings, 1), send(embeddings, -1)
    far_first, far_second = send(below[:cut], 1), send(above[cut:], -1)
    sources = [embeddings, above, far_first, far_second, below]

    packed = pack(embeddings, assign, owner_map, depth, devices, cent_count, capacity)
    routed = exchange(packed.reshape(dp_count, cent_count * capacity, -1)).reshape(
        dp_count, cent_count, capacity, -1
    )
    initial = normalize_rows(init_centroids)
    own_half = lax.dynamic_slice_in_dim(initial, core * half, half, 0)
    other_half = lax.dynamic_slice_in_dim(initial, (1 - core) * half, half, 0)
    block = jnp.concatenate([own_half, other_half])
    scored = [
        score_piece(raws, block, cut, cost, keep)
        for raws, cost, keep in [
            ([embeddings], OWN_COST, True),
            ([above], NEAR_COST, True),
            ([far_first, far_second], FAR_COST, False),
            ([below], NEAR_COST, True),
        ]
    ]
    members = [member for *parts, _, _ in scored for member in parts or [None, None]]
    partial_total = jnp.concatenate([total for *_, total, _ in scored], axis=1)
    scale = jnp.concatenate([scale for *_, scale in scored], axis=1)

    totals = [partial_total] + [send(partial_total, -k) for k in range(1, cent_count)]
    parted = [routed[:, k] for k in range(cent_count)]
    own, for_sibling = weighted_sums(members, sources, scale, totals, block, core, 0, parted[1:])
    both = (own.astype(jnp.float32) + swap_cores(for_sibling).astype(jnp.float32)).astype(jnp.bfloat16)
    arrived = exchange_plane(both.reshape(planes, share, feature_width))

    blocks = [routed, send(parted[1], 1), None, send(parted[3], -1)]
    blocks[2] = send(order(parted[2], [blocks[1], blocks[3]]), 2)

    own_half = exchange_plane(combine(arrived, planes, [])).reshape(half, feature_width)
    members, partial_total = score_rows(sources, scale, own_half, swap_cores(own_half), cut)
    totals = [partial_total] + [send(partial_total, -k) for k in range(1, cent_count)]
    (sums,) = weighted_sums(members, sources, scale, totals, own_half, core, planes, [blocks[2]])
    arrived = exchange(sums.reshape(dp_count, share, feature_width))
    similarity, upper = similarity_of(blocks, depth, 0, 2, None)
    spread = combine(arrived, planes, [upper])
    similarity, lower = similarity_of(blocks, depth, 1, 2, similarity)
    own_half = hold(exchange_plane(spread).reshape(half, feature_width), [lower])
    return (finish(own_half, swap_cores(own_half), core), similarity)


def solution(mesh):
    return jax.shard_map(
        shards,
        mesh=mesh,
        in_specs=(P(AXES, None), P("cent", None), P(AXES), P()),
        out_specs=(P("cent", None), P(AXES, None, None)),
        check_vma=False,
    )
```

```python
import functools
import math

import jax
import jax.numpy as jnp
from jax import lax
from jax.experimental import pallas as pl
from jax.experimental.pallas import tpu as pltpu
from jax.sharding import PartitionSpec as P

ROUNDS = 2
AXES = ("dp", "cent")

epsilon = 1e-06
logit_divisor = 0.02
MIB = 1024 * 1024
LABEL_LANES = 128
NEAR_COST = 1_000_000
OWN_COST = 6_000_000_000
FAR_COST = 50_000_000_000
FULL = 61


def unit(matrix):
    wide = matrix.astype(jnp.float32)
    return wide * (1.0 / jnp.sqrt(jnp.sum(wide * wide, axis=-1, keepdims=True) + epsilon))


def normalize_rows(matrix):
    return unit(matrix).astype(jnp.bfloat16)


def contract_final_axis(left, right):
    return lax.dot_general(
        left, right, (((1,), (1,)), ((), ())), preferred_element_type=jnp.float32
    )


def whole():
    return pl.BlockSpec(memory_space=pltpu.VMEM)


def in_hbm():
    return pl.BlockSpec(memory_space=pl.ANY)


def call(kernel, name, vmem, flops, **options):
    return pl.pallas_call(
        kernel,
        name=name,
        cost_estimate=pl.CostEstimate(flops=int(flops), bytes_accessed=1 << 20, transcendentals=0),
        compiler_params=pltpu.CompilerParams(vmem_limit_bytes=vmem * MIB),
        **options,
    )


def membership_of(block, rows, scale):
    scores = contract_final_axis(block, rows)
    membership = jnp.exp2(scores * (scale * (math.log2(math.e) / logit_divisor)))
    return membership.astype(jnp.bfloat16), jnp.sum(membership, axis=0, keepdims=True)


def piece_kernel(sources, block_ref, *rest):
    raw_refs, member_refs = rest[:sources], rest[sources:-2]
    total_ref, scale_ref = rest[-2:]
    size = member_refs[0].shape[1]
    parts = [(ref, at) for ref in raw_refs for at in range(0, ref.shape[0], size)]
    for i, (ref, start) in enumerate(parts):
        raw = ref[start : start + size]
        at = slice(i * size, (i + 1) * size)
        wide = raw.astype(jnp.float32)
        squares = jnp.sum(wide * wide, axis=-1, keepdims=True) + epsilon
        scale = (1.0 / jnp.sqrt(jnp.broadcast_to(squares, (size, 8)))).T[:1]
        scale_ref[:, at] = scale
        member_refs[i][...], total_ref[:, at] = membership_of(block_ref[...], raw, scale)


def score_piece(raws, block, size, cost):
    rows = sum(raw.shape[0] for raw in raws)
    count = block.shape[0]
    line = jax.ShapeDtypeStruct((1, rows), jnp.float32)
    pieces = rows // size
    return call(
        functools.partial(piece_kernel, len(raws)),
        "score_piece",
        12,
        cost,
        in_specs=[whole()] * (1 + len(raws)),
        out_specs=[whole()] * (pieces + 2),
        out_shape=[jax.ShapeDtypeStruct((count, size), jnp.bfloat16)] * pieces + [line] * 2,
    )(block, *raws)


def fetches(sources, size, taken, sems):
    parts = [
        source.at[pl.ds(at, size)] for source in sources for at in range(0, source.shape[0], size)
    ]
    return [
        pltpu.make_async_copy(part, taken.at[pl.ds(i * size, size)], sems.at[i])
        for i, part in enumerate(parts)
    ]


def score_kernel(pieces, scale_ref, own_ref, other_ref, *rest):
    *sources, total_ref, taken, members, block, in_sem, out_sem = rest
    sources, member_refs = sources[:-pieces], sources[-pieces:]
    half = own_ref.shape[0]
    size = members.shape[2]
    arriving = fetches(sources, size, taken, in_sem)
    for copy in arriving:
        copy.start()
    block[:half], block[half:] = own_ref[...], other_ref[...]
    leaving = []
    for i in range(pieces):
        arriving[i].wait()
        at = slice(i * size, (i + 1) * size)
        members[i], total_ref[:, at] = membership_of(block[...], taken[at], scale_ref[:, at])
        leaving.append(pltpu.make_async_copy(members.at[i], member_refs[i], out_sem.at[i]))
        leaving[-1].start()
    for copy in leaving:
        copy.wait()


def score_rows(sources, scale, own_half, other_half, size):
    pieces = scale.shape[1] // size
    width = sources[0].shape[1]
    count = 2 * own_half.shape[0]
    each = pltpu.SemaphoreType.DMA((pieces,))
    out = call(
        functools.partial(score_kernel, pieces),
        "score_rows",
        FULL,
        NEAR_COST,
        in_specs=[whole()] * 3 + [in_hbm()] * len(sources),
        out_specs=[in_hbm()] * pieces + [whole()],
        out_shape=[jax.ShapeDtypeStruct((count, size), jnp.bfloat16)] * pieces
        + [jax.ShapeDtypeStruct((1, pieces * size), jnp.float32)],
        scratch_shapes=[
            pltpu.VMEM((pieces * size, width), jnp.bfloat16),
            pltpu.VMEM((pieces, count, size), jnp.bfloat16),
            pltpu.VMEM((count, width), jnp.bfloat16),
            each,
            each,
        ],
    )(scale, own_half, other_half, *sources)
    return out[:pieces], out[pieces]


def sum_kernel(pieces, depth, source_count, outs, core_ref, scale_ref, *rest):
    total_refs, rest = rest[:depth], rest[depth:]
    *rest, members, taken, running, member_sem, row_sem = rest
    out_refs = rest[-outs:]
    member_refs, sources = rest[:pieces], rest[pieces : pieces + source_count]
    half = running.shape[0] // 2
    size = members.shape[2]
    arriving = [
        (rows, pltpu.make_async_copy(member_refs[i], members.at[i], member_sem.at[i]))
        for i, rows in enumerate(fetches(sources, size, taken, row_sem))
    ]
    for pair in arriving:
        for copy in pair:
            copy.start()
    for i in range(pieces):
        for copy in arriving[i]:
            copy.wait()
        at = slice(i * size, (i + 1) * size)
        total = total_refs[0][:, at]
        for k in range(1, depth):
            j = (i + pieces - k * (pieces // depth)) % pieces
            total = total + total_refs[k][:, j * size : (j + 1) * size]
        weights = members[i].astype(jnp.float32) * (scale_ref[:, at] / total)
        product = jnp.dot(
            weights.astype(jnp.bfloat16), taken[at], preferred_element_type=jnp.float32
        )
        if i == 0:
            running[...] = product
        else:
            running[...] += product
    own, other = running[:half].astype(jnp.bfloat16), running[half:].astype(jnp.bfloat16)
    if outs == 2:
        out_refs[0][...], out_refs[1][...] = own, other
    else:
        chips, _, share, width = out_refs[0].shape
        out_refs[0][:, core_ref[0]] = own.reshape(chips, share, width)
        out_refs[0][:, 1 - core_ref[0]] = other.reshape(chips, share, width)


def weighted_sums(members, sources, scale, totals, core, chips, after):
    pieces = len(members)
    count, size = members[0].shape
    width = sources[0].shape[1]
    half = count // 2
    shapes = [(chips, 2, half // chips, width)] if chips else [(half, width)] * 2
    return call(
        functools.partial(sum_kernel, pieces, len(totals), len(sources), len(shapes)),
        "weighted_sums",
        FULL,
        2 * pieces * size * width * count,
        in_specs=[pl.BlockSpec(memory_space=pltpu.SMEM)]
        + [whole()] * (1 + len(totals))
        + [in_hbm()] * (pieces + len(sources))
        + [in_hbm()] * len(after),
        out_specs=[whole()] * len(shapes),
        out_shape=[jax.ShapeDtypeStruct(shape, jnp.bfloat16) for shape in shapes],
        scratch_shapes=[
            pltpu.VMEM((pieces, count, size), jnp.bfloat16),
            pltpu.VMEM((pieces * size, width), jnp.bfloat16),
            pltpu.VMEM((count, width), jnp.float32),
            pltpu.SemaphoreType.DMA((pieces,)),
            pltpu.SemaphoreType.DMA((pieces,)),
        ],
    )(core.reshape(1).astype(jnp.int32), scale, *totals, *members, *sources, *after)


def add_kernel(left_ref, right_ref, out_ref):
    total = left_ref[...].astype(jnp.float32) + right_ref[...].astype(jnp.float32)
    out_ref[...] = total.astype(jnp.bfloat16)


def add(left, right):
    return call(
        add_kernel,
        "add",
        8,
        left.size,
        in_specs=[whole()] * 2,
        out_specs=whole(),
        out_shape=jax.ShapeDtypeStruct(left.shape, left.dtype),
    )(left, right)


def combine_kernel(arrived_ref, *rest):
    spread_ref = rest[-1]
    total = arrived_ref[0].astype(jnp.float32)
    for i in range(1, arrived_ref.shape[0]):
        total = total + arrived_ref[i].astype(jnp.float32)
    share = normalize_rows(total)
    for i in range(spread_ref.shape[0]):
        spread_ref[i] = share


def combine(arrived, receivers, after):
    return call(
        combine_kernel,
        "combine",
        8,
        2 * arrived.size,
        in_specs=[whole()] + [in_hbm()] * len(after),
        out_specs=whole(),
        out_shape=jax.ShapeDtypeStruct((receivers,) + arrived.shape[1:], arrived.dtype),
    )(arrived, *after)


def finish_kernel(core_ref, own_ref, other_ref, out_ref):
    half, width = own_ref.shape
    core = core_ref[0]
    for side, ref in ((core, own_ref), (1 - core, other_ref)):
        at = pl.ds(pl.multiple_of(side * half, half), half)
        out_ref[at] = ref[...].astype(jnp.float32) * math.sqrt(width)


def finish(own_half, other_half, core):
    half, width = own_half.shape
    return call(
        finish_kernel,
        "finish",
        8,
        own_half.size,
        in_specs=[pl.BlockSpec(memory_space=pltpu.SMEM), whole(), whole()],
        out_specs=whole(),
        out_shape=jax.ShapeDtypeStruct((2 * half, width), jnp.float32),
    )(core.reshape(1).astype(jnp.int32), own_half, other_half)


def pack_kernel(devices, cent_count, capacity, depth_ref, raw_ref, assign_ref, table_ref, out_ref, rows, place):
    step = pl.program_id(0)
    local_rows, width = raw_ref.shape
    high_count, low_count = table_ref.shape

    @pl.when(step == 0)
    def _():
        rows[:, :width] = normalize_rows(raw_ref[...])
        cluster = assign_ref[...]
        high, low = lax.div(cluster, low_count), lax.rem(cluster, low_count)
        high_hits = lax.broadcasted_iota(jnp.int32, (high_count, local_rows), 0) == high
        by_low = lax.dot_general(
            table_ref[...].astype(jnp.float32).astype(jnp.bfloat16),
            jnp.where(high_hits, 1.0, 0.0).astype(jnp.bfloat16),
            (((0,), (0,)), ((), ())),
            preferred_element_type=jnp.float32,
        )
        low_hits = lax.broadcasted_iota(jnp.int32, (low_count, local_rows), 0) == low
        owner = jnp.sum(jnp.where(low_hits, by_low, 0.0), axis=0, keepdims=True).astype(jnp.int32)
        owner_hits = lax.broadcasted_iota(jnp.int32, (devices, local_rows), 0) == owner
        group = min(128, local_rows)
        earlier = lax.broadcasted_iota(jnp.int32, (group, group), 0) < (
            lax.broadcasted_iota(jnp.int32, (group, group), 1)
        )
        earlier = jnp.where(earlier, 1.0, 0.0).astype(jnp.bfloat16)
        ones = jnp.where(owner_hits, 1.0, 0.0)
        before, seen = [], jnp.zeros((devices, 1), jnp.float32)
        for at in range(0, local_rows, group):
            some = ones[:, at : at + group]
            before.append(
                jnp.dot(some.astype(jnp.bfloat16), earlier, preferred_element_type=jnp.float32) + seen
            )
            seen = seen + jnp.sum(some, axis=1, keepdims=True)
        before = jnp.concatenate(before, axis=1)
        slot = jnp.sum(jnp.where(owner_hits, before, 0.0), axis=0, keepdims=True).astype(jnp.int32)
        owner_dp, owner_depth = lax.div(owner, cent_count), lax.rem(owner, cent_count)
        distance = lax.rem(owner_depth + cent_count - depth_ref[0], cent_count)
        place[...] = (owner_dp * cent_count + distance) * capacity + slot
        number = cluster + 1
        lane = lax.broadcasted_iota(jnp.int32, (LABEL_LANES, local_rows), 0)
        digits = jnp.where(
            lane == 0, lax.div(number, 256), jnp.where(lane == 1, lax.rem(number, 256), 0)
        )
        rows[:, width:] = digits.astype(jnp.float32).T.astype(jnp.bfloat16)

    size = out_ref.shape[0]
    taken = lax.broadcasted_iota(jnp.int32, (size, local_rows), 0) + step * size == place[...]
    taken = jnp.where(taken, 1.0, 0.0).astype(jnp.bfloat16)
    out_ref[...] = jnp.dot(taken, rows[...], preferred_element_type=jnp.float32).astype(jnp.bfloat16)


def pack(embeddings, assign, owner_map, depth, devices, cent_count, capacity):
    local_rows, width = embeddings.shape
    slots = devices * capacity
    tile = min(512, slots)
    low_count = 128
    return call(
        functools.partial(pack_kernel, devices, cent_count, capacity),
        "pack",
        FULL,
        2 * slots * width * local_rows,
        grid=(slots // tile,),
        in_specs=[pl.BlockSpec(memory_space=pltpu.SMEM), whole(), whole(), whole()],
        out_specs=pl.BlockSpec((tile, width + LABEL_LANES), lambda i: (i, 0)),
        out_shape=jax.ShapeDtypeStruct((slots, width + LABEL_LANES), jnp.bfloat16),
        scratch_shapes=[
            pltpu.VMEM((local_rows, width + LABEL_LANES), jnp.bfloat16),
            pltpu.VMEM((1, local_rows), jnp.int32),
        ],
    )(
        depth.reshape(1).astype(jnp.int32),
        embeddings,
        assign.reshape(1, local_rows),
        owner_map.reshape(-1, low_count),
    )


def order_kernel(*refs):
    del refs


def order(value, after):
    return call(
        order_kernel,
        "order",
        FULL,
        1,
        in_specs=[in_hbm()] * (1 + len(after)),
        out_specs=in_hbm(),
        out_shape=jax.ShapeDtypeStruct(value.shape, value.dtype),
        input_output_aliases={0: 0},
    )(value, *after)


def hold_kernel(value_ref, *rest):
    rest[-1][...] = value_ref[...]


def hold(value, after):
    return call(
        hold_kernel,
        "hold",
        8,
        value.size,
        in_specs=[whole()] + [in_hbm()] * len(after),
        out_specs=whole(),
        out_shape=jax.ShapeDtypeStruct(value.shape, value.dtype),
    )(value, *after)


def similarity_kernel(cent_count, first, depth_ref, *rest):
    block_refs = rest[:cent_count]
    out_ref, flag_ref, gathered, column, row, sem = rest[-6:]
    step = pl.program_id(0)
    dp_count, _, capacity, lanes = gathered.shape
    size, slots = out_ref.shape[1:]
    width = lanes - LABEL_LANES

    @pl.when(step == 0)
    def _():
        arriving = []
        for k in range(cent_count):
            source = lax.rem(depth_ref[0] + cent_count - k, cent_count)
            block = block_refs[k].at[:, 0] if k == 0 else block_refs[k]
            arriving.append(pltpu.make_async_copy(block, gathered.at[:, source], sem.at[k]))
            arriving[-1].start()
        for copy in arriving:
            copy.wait()
        digits = gathered[:, :, :, width:].reshape(slots, LABEL_LANES).astype(jnp.float32)
        number = digits[:, 0:1] * 256.0 + digits[:, 1:2]
        column[...] = jnp.where(number > 0.0, number, -1.0)
        across = digits.T
        row[...] = across[0:1] * 256.0 + across[1:2]
        flag_ref[...] = jnp.zeros_like(flag_ref)

    per_step = size // (cent_count * capacity)
    start = pl.multiple_of((first + step) * size, size)
    rows = gathered[pl.ds((first + step) * per_step, per_step), :, :, :width].reshape(size, width)
    every = gathered[:, :, :, :width].reshape(slots, width)
    same = column[pl.ds(start, size)] == row[...]
    out_ref[0] = jnp.where(
        same, contract_final_axis(rows, every) * math.sqrt(width), 0.0
    ).astype(jnp.bfloat16)
    main_diagonal = lax.broadcasted_iota(jnp.int32, (size, size), 0) == (
        lax.broadcasted_iota(jnp.int32, (size, size), 1)
    )
    corner = out_ref[0, :, pl.ds(start, size)]
    out_ref[0, :, pl.ds(start, size)] = jnp.where(
        main_diagonal, 0.0, corner.astype(jnp.float32)
    ).astype(jnp.bfloat16)


def similarity_of(blocks, depth, part, parts, held):
    cent_count = len(blocks)
    dp_count, capacity, lanes = blocks[1].shape
    slots = cent_count * dp_count * capacity
    tile = min(256, slots // parts)
    steps = slots // tile // parts
    aliased = [] if held is None else [held]
    return call(
        functools.partial(similarity_kernel, cent_count, part * steps),
        "similarity",
        FULL,
        2 * slots * slots * lanes // parts,
        grid=(steps,),
        in_specs=[pl.BlockSpec(memory_space=pltpu.SMEM)] + [in_hbm()] * (cent_count + len(aliased)),
        out_specs=[
            pl.BlockSpec((1, tile, slots), lambda i: (0, part * steps + i, 0)),
            pl.BlockSpec((8, 128), lambda i: (0, 0)),
        ],
        out_shape=[
            jax.ShapeDtypeStruct((1, slots, slots), jnp.bfloat16),
            jax.ShapeDtypeStruct((8, 128), jnp.float32),
        ],
        scratch_shapes=[
            pltpu.VMEM((dp_count, cent_count, capacity, lanes), jnp.bfloat16),
            pltpu.VMEM((slots, 1), jnp.float32),
            pltpu.VMEM((1, slots), jnp.float32),
            pltpu.SemaphoreType.DMA((cent_count,)),
        ],
        input_output_aliases={1 + cent_count: 0} if aliased else {},
    )(depth.reshape(1).astype(jnp.int32), *blocks, *aliased)


def shards(embeddings, init_centroids, assign, owner_map):
    devices = lax.axis_size(AXES)
    cent_count = lax.axis_size("cent")
    dp_count = lax.axis_size("dp")
    depth = lax.axis_index("cent")
    local_rows, feature_width = embeddings.shape
    planes = dp_count // 2
    core = lax.axis_index("dp") % 2
    half = init_centroids.shape[0] // 2
    share = half // planes
    capacity = 2 * local_rows // devices
    group_rows = cent_count * local_rows

    def send(value, step):
        return lax.ppermute(
            value, "cent", [(z, (z + step) % cent_count) for z in range(cent_count)]
        )

    def exchange(value):
        return lax.all_to_all(value, "dp", 0, 0, tiled=True)

    same_core = [[2 * chip + c for chip in range(planes)] for c in range(2)]
    other_core = [(i, i + 1 - 2 * (i % 2)) for i in range(dp_count)]

    def exchange_plane(value):
        return lax.all_to_all(value, "dp", 0, 0, axis_index_groups=same_core, tiled=True)

    def swap_cores(value):
        return lax.ppermute(value, "dp", other_core)

    cut = local_rows // 2
    below, above = send(embeddings, 1), send(embeddings, -1)
    far_first, far_second = send(below[:cut], 1), send(above[cut:], -1)
    sources = [embeddings, above, far_first, far_second, below]

    packed = pack(embeddings, assign, owner_map, depth, devices, cent_count, capacity)
    routed = exchange(packed.reshape(dp_count, cent_count * capacity, -1)).reshape(
        dp_count, cent_count, capacity, -1
    )
    initial = normalize_rows(init_centroids)
    own_half = lax.dynamic_slice_in_dim(initial, core * half, half, 0)
    other_half = lax.dynamic_slice_in_dim(initial, (1 - core) * half, half, 0)
    block = jnp.concatenate([own_half, other_half])
    scored = [
        score_piece(raws, block, cut, cost)
        for raws, cost in [
            ([embeddings], OWN_COST),
            ([above], NEAR_COST),
            ([far_first, far_second], FAR_COST),
            ([below], NEAR_COST),
        ]
    ]
    members = [member for *parts, _, _ in scored for member in parts]
    partial_total = jnp.concatenate([total for *_, total, _ in scored], axis=1)
    scale = jnp.concatenate([scale for *_, scale in scored], axis=1)

    totals = [partial_total] + [send(partial_total, -k) for k in range(1, cent_count)]
    parted = [routed[:, k] for k in range(cent_count)]
    own, for_sibling = weighted_sums(members, sources, scale, totals, core, 0, parted[1:])
    both = add(own, swap_cores(for_sibling))
    arrived = exchange_plane(both.reshape(planes, share, feature_width))

    blocks = [routed, send(parted[1], 1), None, send(parted[3], -1)]
    blocks[2] = send(order(parted[2], [blocks[1], blocks[3]]), 2)

    own_half = exchange_plane(combine(arrived, planes, [])).reshape(half, feature_width)
    members, partial_total = score_rows(sources, scale, own_half, swap_cores(own_half), cut)
    totals = [partial_total] + [send(partial_total, -k) for k in range(1, cent_count)]
    (sums,) = weighted_sums(members, sources, scale, totals, core, planes, [blocks[2]])
    arrived = exchange(sums.reshape(dp_count, share, feature_width))
    similarity, upper = similarity_of(blocks, depth, 0, 2, None)
    spread = combine(arrived, planes, [upper])
    similarity, lower = similarity_of(blocks, depth, 1, 2, similarity)
    own_half = hold(exchange_plane(spread).reshape(half, feature_width), [lower])
    return (finish(own_half, swap_cores(own_half), core), similarity)


def solution(mesh):
    return jax.shard_map(
        shards,
        mesh=mesh,
        in_specs=(P(AXES, None), P("cent", None), P(AXES), P()),
        out_specs=(P("cent", None), P(AXES, None, None)),
        check_vma=False,
    )
```
